32 devices in a mesh: dp: 4 (over y, x), expert: 8 (over z, core).
Axes of the slice: x: 2, y: 2, z: 4, core: 2. Of those that a mesh axis runs over, the one named last changes fastest.
Arguments:
- tokens: bfloat16 [4096, 3584], P(('dp', 'expert')), may hold values from -6 to 6
- cotangent: bfloat16 [4096, 3584], P(('dp', 'expert')), may hold values from -0.375 to 0.375
- gate_scale: float32 [4096], P(('dp', 'expert')), may hold values from 0.2 to 1
- expert_index: int32 [4096], P(('dp', 'expert')), may hold values from 0 to 7, as said below
- hot_index: int32 [8], replicated, may hold values from 0 to 7, as said below
- w_gate: bfloat16 [8, 3584, 1024], P('expert', None, 'dp'), may hold values from -0.09375 to 0.09375
- w_up: bfloat16 [8, 3584, 1024], P('expert', None, 'dp'), may hold values from -0.09375 to 0.09375
- w_down: bfloat16 [8, 1024, 3584], P('expert', 'dp'), may hold values from -0.1875 to 0.1875
Outputs:
- grad_gate: bfloat16 [8, 3584, 1024], P('expert', None, 'dp')
- grad_up: bfloat16 [8, 3584, 1024], P('expert', None, 'dp')
- grad_down: bfloat16 [8, 1024, 3584], P('expert', 'dp')
- hot_grads: bfloat16 [1, 3584, 3, 1024], P(None, 'expert', None, 'dp')
The draws below stay inside these ranges and needn't reach their ends.
Inputs may be any that keep to these rules, and one draw needn't show every extreme that they name: `expert_index`: among the 128 tokens of one device (aligned blocks of rows), at most 24 are routed to any one expert other than hot_index[0], and from 24 to 48 to hot_index[0]. In every draw each group of devices sharing a dp index has an expert that receives exactly 24 tokens from each of its devices, and some devices route exactly 48 tokens to hot_index[0]. `hot_index`: A permutation of the 8 experts; its first entry is the replicated expert, to which every device routes at least as many tokens as to any other expert.
All inputs are finite; a program needn't handle non-finite values.
Results may differ from the reference program's by a relative error of at most 0.0058.
Values may be sent and summed in bfloat16 or wider, within the bound.
No kernel may reach another device: no remote copies, remote signals or barrier semaphores. Data moves between devices by JAX's collectives and lax.ppermute only.
A program may use at most 128 MiB of HBM per device.

```python
import jax
import jax.numpy as jnp
from jax import lax

D = 3584
FF = 1024
TOK_DEV = 128
EXPERTS = 8
TOKENS = 4096
CAP = 24
CAP_HOT = 48


def routing_plan(key):
    blocks = TOKENS // TOK_DEV
    row_groups = blocks // EXPERTS
    order = jax.random.permutation(jax.random.fold_in(key, 101), EXPERTS).astype(jnp.int32)
    hot_expert = order[0]
    full_shift = jax.random.randint(jax.random.fold_in(key, 102), (row_groups,), 0, EXPERTS - 1).astype(jnp.int32)
    full_expert = (hot_expert + 1 + full_shift) % EXPERTS
    forced_row = jax.random.randint(jax.random.fold_in(key, 103), (), 0, row_groups).astype(jnp.int32)
    block_row = jnp.arange(blocks, dtype=jnp.int32) // EXPERTS
    hot_count = jax.random.randint(jax.random.fold_in(key, 104), (blocks,), CAP, CAP_HOT + 1).astype(jnp.int32)
    hot_count = jnp.where(block_row == forced_row, CAP_HOT, hot_count)
    expert_grid = jnp.arange(EXPERTS, dtype=jnp.int32)[None, :, None]
    slot_grid = jnp.arange(CAP_HOT, dtype=jnp.int32)[None, None, :]
    is_hot = expert_grid == hot_expert
    usable = jnp.where(is_hot, slot_grid < hot_count[:, None, None], slot_grid < CAP)
    forced = is_hot & usable | (expert_grid == full_expert[block_row][:, None, None]) & (slot_grid < CAP)
    random_score = jax.random.randint(jax.random.fold_in(key, 105), (blocks, EXPERTS, CAP_HOT), 0, 65536).astype(jnp.int32)
    flat_slot = expert_grid * CAP_HOT + slot_grid
    ranking = (random_score + 131072 * forced.astype(jnp.int32)) * (EXPERTS * CAP_HOT) + flat_slot
    ranking = jnp.where(usable, ranking, -1 - flat_slot)
    chosen = lax.top_k(ranking.reshape(blocks, EXPERTS * CAP_HOT), TOK_DEV)[1].astype(jnp.int32)
    shuffle_key = jax.random.randint(jax.random.fold_in(key, 106), (blocks, TOK_DEV), 0, 65536).astype(jnp.int32)
    shuffle_key = shuffle_key * TOK_DEV + jnp.arange(TOK_DEV, dtype=jnp.int32)[None, :]
    shuffle = jnp.argsort(shuffle_key, axis=1).astype(jnp.int32)
    picked = jnp.take_along_axis(chosen, shuffle, axis=1)
    return (order, (picked // CAP_HOT).reshape(TOKENS).astype(jnp.int32))


def draw_expert_index(key, part):
    return routing_plan(key)[1]


def draw_hot_index(key, part):
    return routing_plan(key)[0]


def with_spikes(drawn, rng, source, target, blocks, factor):
    owner, partner = [(jnp.arange(drawn.shape[axis_at]) // (drawn.shape[axis_at] // blocks)).reshape([-1 if axis == axis_at else 1 for axis in range(drawn.ndim)]) for axis_at in (source, target)]
    chosen = jax.random.permutation(rng, blocks)[partner]
    strong = (owner == chosen) | (owner == (partner + blocks // 2) % blocks)
    return jnp.where(strong, factor * drawn, drawn)


def level_of(rng, dims, cuts, smallest, top_value):
    gain, own = 1.0, jax.random.fold_in(rng, 6)
    for axis_at, blocks in cuts:
        steps = jnp.exp(jax.random.uniform(jax.random.fold_in(own, axis_at), (blocks,), jnp.float32, smallest / len(cuts), top_value / len(cuts)))
        gain = gain * jnp.repeat(steps, dims[axis_at] // blocks).reshape([-1 if axis == axis_at else 1 for axis in range(len(dims))])
    return gain


def scatter_about(rng, shape, spread, limit, shards=(), kind=jnp.bfloat16):
    level = level_of(rng, shape, shards, -0.22, 0.18) if shards else 1.0
    array = jax.random.normal(rng, shape, jnp.float32) * spread * level
    return jnp.minimum(jnp.maximum(array, -limit), limit).astype(kind)


def heavy_noise(own_key, shape, spread, limit, split, heavy, kind=jnp.bfloat16):
    entries = spread * jax.random.normal(own_key, shape, jnp.float32)
    if split:
        entries = entries * level_of(own_key, shape, split, -0.22, 0.18)
    return jnp.clip(with_spikes(entries, jax.random.fold_in(own_key, 3), *heavy), -limit, limit).astype(kind)


def setup_inputs(seed: int = 0) -> dict:
    arg_keys = jax.random.split(jax.random.key(seed), 9)
    tokens = heavy_noise(arg_keys[0], (TOKENS, D), 1.0, 6.0, ((0, 32),), (0, 1, 32, 2.75))
    cotangent = scatter_about(arg_keys[1], (TOKENS, D), 0.0625, 0.375, ((0, 32),))
    gate_scale = jnp.clip(0.2 + 0.8 * jax.random.uniform(arg_keys[2], (TOKENS,), jnp.float32) ** level_of(arg_keys[2], (TOKENS,), ((0, 32),), -0.2, 0.2), 0.2, 1.0)
    expert_index = draw_expert_index(jax.random.fold_in(arg_keys[8], 71), 0)
    hot_index = draw_hot_index(jax.random.fold_in(arg_keys[8], 71), 0)
    w_gate = scatter_about(arg_keys[5], (EXPERTS, D, FF), D ** -0.5, 0.09375, ((0, 8), (2, 4)))
    w_up = scatter_about(arg_keys[6], (EXPERTS, D, FF), D ** -0.5, 0.09375, ((0, 8), (2, 4)))
    w_down = scatter_about(arg_keys[7], (EXPERTS, FF, D), FF ** -0.5, 0.1875, ((0, 8), (1, 4)))
    return dict(tokens=tokens, cotangent=cotangent, gate_scale=gate_scale, expert_index=expert_index, hot_index=hot_index, w_gate=w_gate, w_up=w_up, w_down=w_down)


def expert_terms(row_tokens, row_grads, gate_matrix, up_matrix, down_matrix):
    pre_gate = jnp.dot(row_tokens, gate_matrix, preferred_element_type=jnp.float32)
    pre_up = jnp.dot(row_tokens, up_matrix, preferred_element_type=jnp.float32)
    hidden_back = jnp.dot(row_grads, down_matrix.T, preferred_element_type=jnp.float32)
    sigmoid_gate = jax.nn.sigmoid(pre_gate)
    activated = pre_gate * sigmoid_gate
    hidden = (activated * pre_up).astype(jnp.bfloat16)
    gate_grad = (hidden_back * pre_up * sigmoid_gate * (1.0 + pre_gate * (1.0 - sigmoid_gate))).astype(jnp.bfloat16)
    up_grad = (hidden_back * activated).astype(jnp.bfloat16)
    return hidden, gate_grad, up_grad


def pick_rows(chosen, tokens, route_grad, limit_rows):
    row_index = jnp.nonzero(chosen, size=limit_rows, fill_value=0)[0].astype(jnp.int32)
    live_count = jnp.sum(chosen.astype(jnp.int32))
    is_live = (jnp.arange(limit_rows, dtype=jnp.int32) < live_count)[:, None]
    nothing = jnp.zeros((), tokens.dtype)
    return jnp.where(is_live, tokens[row_index], nothing), jnp.where(is_live, route_grad[row_index], nothing)


def reference(tokens, cotangent, gate_scale, expert_index, hot_index, w_gate, w_up, w_down):
    hot_expert = hot_index[0]
    route_grad = (gate_scale[:, None] * cotangent.astype(jnp.float32)).astype(jnp.bfloat16)
    blocks = TOKENS // TOK_DEV

    def one_expert(expert):
        chosen = (expert_index == expert) & (expert_index != hot_expert)
        row_tokens, row_grads = pick_rows(chosen, tokens, route_grad, CAP * blocks)
        hidden, gate_grad, up_grad = expert_terms(row_tokens, row_grads, w_gate[expert], w_up[expert], w_down[expert])
        gate_total = jnp.dot(row_tokens.T, gate_grad, preferred_element_type=jnp.float32)
        up_total = jnp.dot(row_tokens.T, up_grad, preferred_element_type=jnp.float32)
        down_total = jnp.dot(hidden.T, row_grads, preferred_element_type=jnp.float32)
        return gate_total.astype(jnp.bfloat16), up_total.astype(jnp.bfloat16), down_total.astype(jnp.bfloat16)

    grad_gate, grad_up, grad_down = lax.map(one_expert, jnp.arange(EXPERTS, dtype=jnp.int32))
    row_tokens, row_grads = pick_rows(expert_index == hot_expert, tokens, route_grad, CAP_HOT * blocks)
    hidden, gate_grad, up_grad = expert_terms(row_tokens, row_grads, w_gate[hot_expert], w_up[hot_expert], w_down[hot_expert])
    gate_total = jnp.dot(row_tokens.T, gate_grad, preferred_element_type=jnp.float32)
    up_total = jnp.dot(row_tokens.T, up_grad, preferred_element_type=jnp.float32)
    down_total = jnp.dot(row_grads.T, hidden, preferred_element_type=jnp.float32)
    hot_grads = jnp.stack([gate_total, up_total, down_total], axis=1).astype(jnp.bfloat16)[None]
    return grad_gate, grad_up, grad_down, hot_grads
```

```python
import functools

import jax
import jax.numpy as jnp
from jax import lax
from jax.experimental import pallas as pl
from jax.experimental.pallas import tpu as pltpu
from jax.sharding import PartitionSpec as P

CONTRACT_ROWS = (((0,), (0,)), ((), ()))


def spread(block, axis, source):
    block = jnp.where(lax.axis_index(axis) == source, block, jnp.zeros_like(block))
    return lax.psum(block, axis)


def expert_terms(row_tokens, row_grads, gate_matrix, up_matrix, down_matrix):
    pre_gate = jnp.dot(row_tokens, gate_matrix, preferred_element_type=jnp.float32)
    pre_up = jnp.dot(row_tokens, up_matrix, preferred_element_type=jnp.float32)
    hidden_back = lax.dot_general(
        row_grads, down_matrix, (((1,), (1,)), ((), ())), preferred_element_type=jnp.float32
    )
    sigmoid_gate = jax.nn.sigmoid(pre_gate)
    activated = pre_gate * sigmoid_gate
    hidden = (activated * pre_up).astype(jnp.bfloat16)
    gate_grad = (
        hidden_back * pre_up * sigmoid_gate * (1.0 + pre_gate * (1.0 - sigmoid_gate))
    ).astype(jnp.bfloat16)
    up_grad = (hidden_back * activated).astype(jnp.bfloat16)
    return (hidden, gate_grad, up_grad)


def column_sum(left, right):
    return lax.dot_general(left, right, CONTRACT_ROWS, preferred_element_type=jnp.float32)


def route_rows(selector, values):
    return jnp.dot(selector, values, preferred_element_type=jnp.float32).astype(jnp.bfloat16)


def on_large_mesh(tokens, cotangent, gate_scale, expert_index, hot_index, w_gate, w_up, w_down):
    tok_rows, feature_width = tokens.shape
    experts = lax.axis_size("expert")
    capacity = 3 * tok_rows // (2 * experts)
    hot_capacity = 2 * capacity
    hot_expert = hot_index[0]
    route_grad = (gate_scale[:, None] * cotangent.astype(jnp.float32)).astype(jnp.bfloat16)
    is_hot = expert_index == hot_expert
    not_hot = jnp.logical_not(is_hot)
    owners = lax.broadcasted_iota(jnp.int32, (tok_rows, experts), 1)
    member = ((expert_index[:, None] == owners) & not_hot[:, None]).astype(jnp.int32)
    bucket_place = jnp.sum((jnp.cumsum(member, axis=0) - 1) * member, axis=1)
    slot_index = expert_index * capacity + bucket_place
    slot_grid = lax.broadcasted_iota(jnp.int32, (experts * capacity, tok_rows), 0)
    cold_map = ((slot_grid == slot_index[None, :]) & not_hot[None, :]).astype(jnp.bfloat16)
    hot_place = jnp.cumsum(is_hot.astype(jnp.int32)) - 1
    hot_grid = lax.broadcasted_iota(jnp.int32, (hot_capacity, tok_rows), 0)
    hot_map = ((hot_grid == hot_place[None, :]) & is_hot[None, :]).astype(jnp.bfloat16)
    send_tokens = route_rows(cold_map, tokens).reshape(experts, capacity, feature_width)
    send_grads = route_rows(cold_map, route_grad).reshape(experts, capacity, feature_width)
    own_hot_tokens = route_rows(hot_map, tokens)
    own_hot_grads = route_rows(hot_map, route_grad)
    arrived_tokens, arrived_grads = (
        lax.all_to_all(send_tokens, "expert", split_axis=0, concat_axis=0, tiled=True),
        lax.all_to_all(send_grads, "expert", split_axis=0, concat_axis=0, tiled=True),
    )
    cold_tokens, cold_grads, hot_tokens, hot_row_grads = (
        lax.all_gather(
            arrived_tokens.reshape(experts * capacity, feature_width), "dp", axis=0, tiled=True
        ),
        lax.all_gather(
            arrived_grads.reshape(experts * capacity, feature_width), "dp", axis=0, tiled=True
        ),
        lax.all_gather(own_hot_tokens, "dp", axis=0, tiled=True),
        lax.all_gather(own_hot_grads, "dp", axis=0, tiled=True),
    )
    shadow_gate, shadow_up, shadow_down = (
        spread(w_gate[0], "expert", hot_expert),
        spread(w_up[0], "expert", hot_expert),
        spread(w_down[0], "expert", hot_expert),
    )
    hidden, gate_grad, up_grad = expert_terms(
        cold_tokens, cold_grads, w_gate[0], w_up[0], w_down[0]
    )
    grad_gate = column_sum(cold_tokens, gate_grad).astype(jnp.bfloat16)
    grad_up = column_sum(cold_tokens, up_grad).astype(jnp.bfloat16)
    grad_down = column_sum(hidden, cold_grads).astype(jnp.bfloat16)
    hot_hidden, hot_gate_grad, hot_up_grad = expert_terms(
        hot_tokens, hot_row_grads, shadow_gate, shadow_up, shadow_down
    )
    gate_part = column_sum(hot_tokens, hot_gate_grad)
    up_part = column_sum(hot_tokens, hot_up_grad)
    down_part = column_sum(hot_row_grads, hot_hidden)
    owned_part = lax.psum_scatter(
        jnp.stack([gate_part, up_part, down_part], axis=1),
        "expert",
        scatter_dimension=0,
        tiled=True,
    )
    hot_grads = owned_part.astype(jnp.bfloat16)[None]
    return (grad_gate[None], grad_up[None], grad_down[None], hot_grads)


ANYWHERE = pl.BlockSpec(memory_space=pl.ANY)
VMEM_LIMIT = 56 * 2**20


def together(*arrays):
    return pl.pallas_call(
        lambda *refs: None,
        out_shape=[jax.ShapeDtypeStruct(a.shape, a.dtype) for a in arrays],
        in_specs=[ANYWHERE] * len(arrays),
        out_specs=[ANYWHERE] * len(arrays),
        input_output_aliases={i: i for i in range(len(arrays))},
        name="together",
    )(*arrays)


def divisor(size, most, unit):
    return max(d for d in range(unit, most + 1, unit) if size % d == 0)


def terms_kernel(plan, hot, chips, n_sources, block_rows, block_columns, *refs):
    flags, mine, theirs = refs[0], refs[1 : 1 + n_sources], refs[1 + n_sources : 1 + 2 * n_sources]
    gate_ref, up_ref, down_ref = refs[1 + 2 * n_sources : 4 + 2 * n_sources]
    rest = refs[4 + 2 * n_sources :]
    n_out = 6 if hot else 3
    outs = rest[:n_out]
    tok, grd, gate_w, up_w, down_w, gate_up_t, hidden_t, res_a, res_b, res_c, in_sem, w_sem, out_sem = rest[n_out:]
    rows, width = tok.shape
    hidden_width = gate_w.shape[1]
    core = flags[0]

    def copies(choice, core_value):
        at, result = 0, []
        for k, (source, first, count) in enumerate(plan[choice]):
            own, other = (mine, theirs) if core_value == 0 else (theirs, mine)
            for kind, (ref, buffer) in enumerate(((own, tok), (other, grd))):
                result.append(
                    pltpu.make_async_copy(
                        ref[source].at[pl.ds(first, count)],
                        buffer.at[pl.ds(at, count)],
                        in_sem.at[2 * k + kind],
                    )
                )
            at += count
        return result

    def output(wanted):
        column_blocks = width // block_columns
        if not hot:
            for i in range(column_blocks):
                span = pl.ds(i * block_columns, block_columns)
                yield pltpu.make_async_copy(res_a.at[span], outs[0].at[span], out_sem.at[i])
                yield pltpu.make_async_copy(
                    res_b.at[span], outs[1].at[span], out_sem.at[column_blocks + i]
                )
            yield pltpu.make_async_copy(res_c, outs[2], out_sem.at[2 * column_blocks])
            return
        part = width // (2 * chips)
        for q, res in enumerate((res_a, res_b, res_c)):
            for z in range(chips):
                for c in range(2):
                    yield pltpu.make_async_copy(
                        res.at[pl.ds((2 * z + c) * part, part)],
                        outs[2 * q + (c != wanted)].at[z],
                        out_sem.at[(q * chips + z) * 2 + c],
                    )

    def work():
        weights = [
            pltpu.make_async_copy(w, buffer, w_sem.at[i])
            for i, (w, buffer) in enumerate(((gate_ref, gate_w), (up_ref, up_w), (down_ref, down_w)))
        ]
        for copy in weights:
            copy.start()
        for choice in range(len(plan)):
            for core_value in range(2):

                @pl.when((flags[2] == choice) & (core == core_value))
                def _():
                    for copy in copies(choice, core_value):
                        copy.start()

        for copy in weights:
            copy.wait()
        waits = copies(0, 0)
        sizes = [count for _, _, count in plan[0]]
        arrived = 0
        for block in range(rows // block_rows):
            while sum(sizes[:arrived]) < (block + 1) * block_rows:
                waits[2 * arrived].wait()
                waits[2 * arrived + 1].wait()
                arrived += 1
            span = pl.ds(block * block_rows, block_rows)
            row_tokens, row_grads = tok[span, :], grd[span, :]
            pre_gate = jnp.dot(row_tokens, gate_w[...], preferred_element_type=jnp.float32)
            pre_up = jnp.dot(row_tokens, up_w[...], preferred_element_type=jnp.float32)
            hidden_back = lax.dot_general(
                row_grads, down_w[...], (((1,), (1,)), ((), ())), preferred_element_type=jnp.float32
            )
            sigmoid_gate = jax.nn.sigmoid(pre_gate)
            activated = pre_gate * sigmoid_gate
            hidden = activated * pre_up
            gate_grad = hidden_back * pre_up * sigmoid_gate * (1.0 + pre_gate * (1.0 - sigmoid_gate))
            up_grad = hidden_back * activated
            hidden_t[:, span] = hidden.T.astype(jnp.bfloat16)
            gate_up_t[pl.ds(0, hidden_width), span] = gate_grad.T.astype(jnp.bfloat16)
            gate_up_t[pl.ds(hidden_width, hidden_width), span] = up_grad.T.astype(jnp.bfloat16)

        def columns(i, carry):
            span = pl.ds(pl.multiple_of(i * block_columns, block_columns), block_columns)
            sums = jnp.dot(gate_up_t[...], tok[:, span], preferred_element_type=jnp.float32)
            sums = sums.T.astype(jnp.bfloat16)
            res_a[span, :] = sums[:, :hidden_width]
            res_b[span, :] = sums[:, hidden_width:]
            downs = jnp.dot(hidden_t[...], grd[:, span], preferred_element_type=jnp.float32)
            if hot:
                res_c[span, :] = downs.T.astype(jnp.bfloat16)
            else:
                res_c[:, span] = downs.astype(jnp.bfloat16)
            return carry

        lax.fori_loop(0, width // block_columns, columns, 0)

    if hot:
        for core_value in range(2):

            @pl.when((flags[1] == 1) & (core == core_value))
            def _():
                if core_value == 0:
                    work()
                else:
                    work()
                sent = list(output(core_value))
                for copy in sent:
                    copy.start()
                for copy in sent:
                    copy.wait()

    else:

        @pl.when(flags[1] == 1)
        def _():
            work()

        @pl.when(flags[1] == 0)
        def _():
            for res in (res_a, res_b, res_c):
                res[...] = jnp.zeros_like(res)

        sent = list(output(None))
        for copy in sent:
            copy.start()
        for copy in sent:
            copy.wait()


def expert_call(flags, plan, hot, chips, mine, theirs, gate, up, down):
    width, hidden_width = gate.shape
    rows = sum(count for _, _, count in plan[0])
    block_rows = divisor(rows, 384, 128)
    block_columns = divisor(width, 512, 128)
    part = width // (2 * chips)
    if hot:
        out_shape = [jax.ShapeDtypeStruct((chips, part, hidden_width), jnp.bfloat16)] * 6
        n_out_copies = 6 * chips
    else:
        out_shape = [
            jax.ShapeDtypeStruct((width, hidden_width), jnp.bfloat16),
            jax.ShapeDtypeStruct((width, hidden_width), jnp.bfloat16),
            jax.ShapeDtypeStruct((hidden_width, width), jnp.bfloat16),
        ]
        n_out_copies = 2 * (width // block_columns) + 1
    last = (width, hidden_width) if hot else (hidden_width, width)
    kernel = functools.partial(
        terms_kernel, plan, hot, chips, len(mine), block_rows, block_columns
    )
    return pl.pallas_call(
        kernel,
        out_shape=out_shape,
        in_specs=[pl.BlockSpec(memory_space=pltpu.SMEM)] + [ANYWHERE] * (2 * len(mine) + 3),
        out_specs=[ANYWHERE] * len(out_shape),
        scratch_shapes=[
            pltpu.VMEM((rows, width), jnp.bfloat16),
            pltpu.VMEM((rows, width), jnp.bfloat16),
            pltpu.VMEM((width, hidden_width), jnp.bfloat16),
            pltpu.VMEM((width, hidden_width), jnp.bfloat16),
            pltpu.VMEM((hidden_width, width), jnp.bfloat16),
            pltpu.VMEM((2 * hidden_width, rows), jnp.bfloat16),
            pltpu.VMEM((hidden_width, rows), jnp.bfloat16),
            pltpu.VMEM((width, hidden_width), jnp.bfloat16),
            pltpu.VMEM((width, hidden_width), jnp.bfloat16),
            pltpu.VMEM(last, jnp.bfloat16),
            pltpu.SemaphoreType.DMA((2 * len(plan[0]),)),
            pltpu.SemaphoreType.DMA((3,)),
            pltpu.SemaphoreType.DMA((n_out_copies,)),
        ],
        compiler_params=pltpu.CompilerParams(vmem_limit_bytes=VMEM_LIMIT),
        cost_estimate=pl.CostEstimate(
            flops=12 * rows * width * hidden_width,
            bytes_accessed=4 * rows * width + 12 * width * hidden_width,
            transcendentals=rows * hidden_width,
        ),
        name="hot_terms" if hot else "cold_terms",
    )(flags, *mine, *theirs, gate, up, down)


def on_device(tokens, cotangent, gate_scale, expert_index, hot_index, w_gate, w_up, w_down):
    tok_rows, width = tokens.shape
    experts = lax.axis_size("expert")
    dp = lax.axis_size("dp")
    chips = experts // 2
    capacity = 3 * tok_rows // (2 * experts)
    if chips != 4 or dp != 4 or capacity % 8 != 0:
        return on_large_mesh(
            tokens, cotangent, gate_scale, expert_index, hot_index, w_gate, w_up, w_down
        )
    hot_expert = hot_index[0]
    me = lax.axis_index("expert")
    core, chip = me % 2, me // 2
    flat = [(i, j) for i in range(dp) for j in range(experts)]

    def place_of(i, j):
        return i * experts + j

    def swap(array):
        return lax.ppermute(array, "expert", [(j, j ^ 1) for j in range(experts)])

    def along(array, step):
        return lax.ppermute(array, "expert", [(j, j ^ (2 * step)) for j in range(experts)])

    def first_way(array):
        pairs = [(place_of(i, j), place_of(i ^ (2 if j % 2 else 1), j)) for i, j in flat]
        return lax.ppermute(array, ("dp", "expert"), pairs)

    def second_way(array):
        pairs = [(place_of(i, j), place_of(i ^ (1 if j % 2 else 2), j)) for i, j in flat]
        return lax.ppermute(array, ("dp", "expert"), pairs)

    route_grad = (gate_scale[:, None] * cotangent.astype(jnp.float32)).astype(jnp.bfloat16)
    own = jnp.where(core == 0, tokens, route_grad)
    other = jnp.where(core == 0, route_grad, tokens)
    sibling, sibling_index = swap(other), swap(expert_index)
    earlier = lax.broadcasted_iota(jnp.int32, (tok_rows, tok_rows), 1) < lax.broadcasted_iota(
        jnp.int32, (tok_rows, tok_rows), 0
    )

    def places(index):
        return jnp.sum(((index[:, None] == index[None, :]) & earlier).astype(jnp.int32), axis=1)

    index = jnp.concatenate([expert_index, sibling_index])
    place = jnp.concatenate([places(expert_index), places(sibling_index)])
    holder = jnp.concatenate([jnp.full((tok_rows,), core), jnp.full((tok_rows,), 1 - core)])
    values = jnp.concatenate([own, sibling], axis=0)
    message = 2 * capacity
    slots = lax.broadcasted_iota(jnp.int32, (message, 2 * tok_rows), 0)

    def selector(kind, step):
        target = chip ^ step
        expert = jnp.where(hot_expert // 2 == target, hot_expert, 2 * target)
        offset = 0
        if kind == "second":
            expert = expert ^ 1
        elif kind == "rest":
            expert, offset = hot_expert, capacity
        taken = (index == expert) & (place >= offset) & (place < offset + capacity)
        slot = place - offset + capacity * holder
        return ((slots == slot[None, :]) & taken[None, :]).astype(jnp.bfloat16)

    def rows(*wanted):
        return route_rows(jnp.concatenate([selector(*w) for w in wanted], axis=0), values)

    near_unit = rows(("first", 0), ("rest", 0))
    sent = {k: [rows((k, s)) for s in range(1, chips)] for k in ("first", "rest", "second")}
    own_second = rows(("second", 0))

    near_1, side_1 = first_way(near_unit), second_way(near_unit)
    got = [along(block, s) for s, block in enumerate(sent["first"], 1)]
    first_unit = jnp.concatenate(got, axis=0)
    near_unit, near_1, side_1, first_unit, *sent["rest"] = together(
        near_unit, near_1, side_1, first_unit, *sent["rest"]
    )
    far_1 = second_way(near_1)
    near_2, side_2 = first_way(first_unit), second_way(first_unit)
    got = [along(block, s) for s, block in enumerate(sent["rest"], 1)]
    swapped_1 = [swap(a) for a in (near_unit, side_1, near_1)]
    rest_unit = jnp.concatenate(got, axis=0)
    far_1, first_unit, near_2, side_2, rest_unit, *sent["second"] = together(
        far_1, first_unit, near_2, side_2, rest_unit, *sent["second"]
    )
    far_2 = second_way(near_2)
    near_3, side_3 = first_way(rest_unit), second_way(rest_unit)
    got = [along(block, s) for s, block in enumerate(sent["second"], 1)]
    swapped_1.append(swap(far_1))
    swapped_2 = [swap(a) for a in (first_unit, side_2, near_2)]
    second_unit = jnp.concatenate([own_second] + got, axis=0)
    far_2, rest_unit, near_3, side_3, second_unit = together(
        far_2, rest_unit, near_3, side_3, second_unit
    )
    far_3 = second_way(near_3)
    swapped_2.append(swap(far_2))
    swapped_3 = [swap(a) for a in (rest_unit, side_3, near_3)]
    far_3, second_unit = together(far_3, second_unit)
    near_4, side_4 = first_way(second_unit), second_way(second_unit)
    swapped_3.append(swap(far_3))

    units_1 = [near_unit, near_1, side_1, far_1]
    units_2 = [first_unit, near_2, side_2, far_2]
    units_3 = [rest_unit, near_3, side_3, far_3]
    gate, up, down = w_gate[0], w_up[0], w_down[0]
    is_owner = me == hot_expert
    count_1, count_2, count_4 = 2 * message, (chips - 1) * message, chips * message
    hot_plan = (
        tuple((k, 0, count_1) for k in range(4))
        + tuple((4 + k, 0, count_2) for k in range(4))
        + tuple((8 + k, 0, count_2) for k in range(4))
    )
    flags = jnp.stack([core, is_owner.astype(jnp.int32), jnp.zeros((), jnp.int32)])
    hot = expert_call(
        flags,
        (hot_plan,),
        True,
        chips,
        units_1 + units_2 + units_3,
        swapped_1 + swapped_2 + swapped_3,
        gate,
        up,
        down,
    )

    on_owner_chip = hot_expert // 2 == chip
    owned = []
    for q in range(3):
        kept, given = hot[2 * q], hot[2 * q + 1]
        kept = jnp.where(is_owner, kept, swap(given))

        def block(at, kept=kept):
            return lax.dynamic_index_in_dim(
                kept, jnp.clip(at, 0, chips - 1), 0, keepdims=False
            )

        upward = downward = None
        for step in range(1, chips):
            reach = chips - step
            ups = [(j, j + 2) for j in range(0, 2 * step)]
            downs = [(experts - 1 - j, experts - 3 - j) for j in range(0, 2 * step)]
            sent_up, sent_down = block(chip + reach), block(chip - reach)
            if step > 1:
                sent_up = jnp.where(on_owner_chip, sent_up, upward)
                sent_down = jnp.where(on_owner_chip, sent_down, downward)
            upward = lax.ppermute(sent_up, "expert", ups)
            downward = lax.ppermute(sent_down, "expert", downs)
        arrived = jnp.where(hot_expert // 2 < chip, upward, downward)
        owned.append(jnp.where(on_owner_chip, block(chip), arrived))
    hot_grads = jnp.stack(owned, axis=1)

    far_4 = second_way(near_4)
    units_4 = [second_unit, near_4, side_4, far_4]
    swapped_4 = [swap(a) for a in (second_unit, side_4, near_4, far_4)]
    first_of_chip = jnp.where(on_owner_chip, hot_expert % 2, 0)
    cold_plans = (
        tuple((k, 0, message) for k in range(4)) + tuple((4 + k, 0, count_2) for k in range(4)),
        tuple((8 + k, 0, message) for k in range(4))
        + tuple((8 + k, message, count_2) for k in range(4)),
    )
    flags = jnp.stack(
        [core, jnp.logical_not(is_owner).astype(jnp.int32), (first_of_chip != core).astype(jnp.int32)]
    )
    grad_gate, grad_up, grad_down = expert_call(
        flags,
        cold_plans,
        False,
        chips,
        units_1 + units_2 + units_4,
        swapped_1 + swapped_2 + swapped_4,
        gate,
        up,
        down,
    )
    return (grad_gate[None], grad_up[None], grad_down[None], hot_grads[None])


def solution(mesh):
    placed = (
        P(("dp", "expert"), None),
        P(("dp", "expert"), None),
        P(("dp", "expert")),
        P(("dp", "expert")),
        P(),
        P("expert", None, "dp"),
        P("expert", None, "dp"),
        P("expert", "dp", None),
    )
    return jax.shard_map(
        on_device,
        mesh=mesh,
        in_specs=placed,
        out_specs=(
            P("expert", None, "dp"),
            P("expert", None, "dp"),
            P("expert", "dp", None),
            P(None, "expert", None, "dp"),
        ),
        check_vma=False,
    )
```

```python
import functools

import jax
import jax.numpy as jnp
from jax import lax
from jax.experimental import pallas as pl
from jax.experimental.pallas import tpu as pltpu
from jax.sharding import PartitionSpec as P

CONTRACT_ROWS = (((0,), (0,)), ((), ()))


def spread(block, axis, source):
    block = jnp.where(lax.axis_index(axis) == source, block, jnp.zeros_like(block))
    return lax.psum(block, axis)


def expert_terms(row_tokens, row_grads, gate_matrix, up_matrix, down_matrix):
    pre_gate = jnp.dot(row_tokens, gate_matrix, preferred_element_type=jnp.float32)
    pre_up = jnp.dot(row_tokens, up_matrix, preferred_element_type=jnp.float32)
    hidden_back = lax.dot_general(
        row_grads, down_matrix, (((1,), (1,)), ((), ())), preferred_element_type=jnp.float32
    )
    sigmoid_gate = jax.nn.sigmoid(pre_gate)
    activated = pre_gate * sigmoid_gate
    hidden = (activated * pre_up).astype(jnp.bfloat16)
    gate_grad = (
        hidden_back * pre_up * sigmoid_gate * (1.0 + pre_gate * (1.0 - sigmoid_gate))
    ).astype(jnp.bfloat16)
    up_grad = (hidden_back * activated).astype(jnp.bfloat16)
    return (hidden, gate_grad, up_grad)


def column_sum(left, right):
    return lax.dot_general(left, right, CONTRACT_ROWS, preferred_element_type=jnp.float32)


def route_rows(selector, values):
    return jnp.dot(selector, values, preferred_element_type=jnp.float32).astype(jnp.bfloat16)


def on_large_mesh(tokens, cotangent, gate_scale, expert_index, hot_index, w_gate, w_up, w_down):
    tok_rows, feature_width = tokens.shape
    experts = lax.axis_size("expert")
    capacity = 3 * tok_rows // (2 * experts)
    hot_capacity = 2 * capacity
    hot_expert = hot_index[0]
    route_grad = (gate_scale[:, None] * cotangent.astype(jnp.float32)).astype(jnp.bfloat16)
    is_hot = expert_index == hot_expert
    not_hot = jnp.logical_not(is_hot)
    owners = lax.broadcasted_iota(jnp.int32, (tok_rows, experts), 1)
    member = ((expert_index[:, None] == owners) & not_hot[:, None]).astype(jnp.int32)
    bucket_place = jnp.sum((jnp.cumsum(member, axis=0) - 1) * member, axis=1)
    slot_index = expert_index * capacity + bucket_place
    slot_grid = lax.broadcasted_iota(jnp.int32, (experts * capacity, tok_rows), 0)
    cold_map = ((slot_grid == slot_index[None, :]) & not_hot[None, :]).astype(jnp.bfloat16)
    hot_place = jnp.cumsum(is_hot.astype(jnp.int32)) - 1
    hot_grid = lax.broadcasted_iota(jnp.int32, (hot_capacity, tok_rows), 0)
    hot_map = ((hot_grid == hot_place[None, :]) & is_hot[None, :]).astype(jnp.bfloat16)
    send_tokens = route_rows(cold_map, tokens).reshape(experts, capacity, feature_width)
    send_grads = route_rows(cold_map, route_grad).reshape(experts, capacity, feature_width)
    own_hot_tokens = route_rows(hot_map, tokens)
    own_hot_grads = route_rows(hot_map, route_grad)
    arrived_tokens, arrived_grads = (
        lax.all_to_all(send_tokens, "expert", split_axis=0, concat_axis=0, tiled=True),
        lax.all_to_all(send_grads, "expert", split_axis=0, concat_axis=0, tiled=True),
    )
    cold_tokens, cold_grads, hot_tokens, hot_row_grads = (
        lax.all_gather(
            arrived_tokens.reshape(experts * capacity, feature_width), "dp", axis=0, tiled=True
        ),
        lax.all_gather(
            arrived_grads.reshape(experts * capacity, feature_width), "dp", axis=0, tiled=True
        ),
        lax.all_gather(own_hot_tokens, "dp", axis=0, tiled=True),
        lax.all_gather(own_hot_grads, "dp", axis=0, tiled=True),
    )
    shadow_gate, shadow_up, shadow_down = (
        spread(w_gate[0], "expert", hot_expert),
        spread(w_up[0], "expert", hot_expert),
        spread(w_down[0], "expert", hot_expert),
    )
    hidden, gate_grad, up_grad = expert_terms(
        cold_tokens, cold_grads, w_gate[0], w_up[0], w_down[0]
    )
    grad_gate = column_sum(cold_tokens, gate_grad).astype(jnp.bfloat16)
    grad_up = column_sum(cold_tokens, up_grad).astype(jnp.bfloat16)
    grad_down = column_sum(hidden, cold_grads).astype(jnp.bfloat16)
    hot_hidden, hot_gate_grad, hot_up_grad = expert_terms(
        hot_tokens, hot_row_grads, shadow_gate, shadow_up, shadow_down
    )
    gate_part = column_sum(hot_tokens, hot_gate_grad)
    up_part = column_sum(hot_tokens, hot_up_grad)
    down_part = column_sum(hot_row_grads, hot_hidden)
    owned_part = lax.psum_scatter(
        jnp.stack([gate_part, up_part, down_part], axis=1),
        "expert",
        scatter_dimension=0,
        tiled=True,
    )
    hot_grads = owned_part.astype(jnp.bfloat16)[None]
    return (grad_gate[None], grad_up[None], grad_down[None], hot_grads)


ANYWHERE = pl.BlockSpec(memory_space=pltpu.HBM)
VMEM_LIMIT = 56 * 2**20


def together(passed, awaited=()):
    n = len(passed)
    return pl.pallas_call(
        lambda *refs: None,
        out_shape=[jax.ShapeDtypeStruct(a.shape, a.dtype) for a in passed],
        in_specs=[pl.BlockSpec(memory_space=pl.ANY)] * (n + len(awaited)),
        out_specs=[pl.BlockSpec(memory_space=pl.ANY)] * n,
        input_output_aliases={i: i for i in range(n)},
        name="together",
    )(*passed, *awaited)


def divisor(size, most, unit):
    return max(d for d in range(unit, most + 1, unit) if size % d == 0)


def terms_kernel(kind, plan, n_sources, block_rows, block_columns, *refs):
    flags, refs = refs[0], refs[1:]
    sources, refs = refs[:n_sources], refs[n_sources:]
    weight_refs, refs = refs[:3], refs[3:]
    in_sem, w_sem, out_sem = refs[-3:]
    refs = refs[:-3]
    if kind == "cold":
        *outs, done, tok, grd, gate_w, up_w, down_w, gate_up_t, hidden_t, res_a, res_b, res_c = refs
    else:
        *outs, tok, grd, gate_w, up_w, down_w, gate_up_t, hidden_t, res_a, res_b, res_c = refs
    rows, width = tok.shape
    hidden_width = gate_w.shape[1]
    core = flags[0]
    column_blocks = width // block_columns

    def copies(choice, core_value, first_piece, last_piece):
        at, result = 0, []
        for k, (by_core, count) in enumerate(plan[choice]):
            if first_piece <= k < last_piece:
                for which, buffer in enumerate((tok, grd)):
                    source, first = by_core[core_value][which]
                    result.append(
                        pltpu.make_async_copy(
                            sources[source].at[pl.ds(first, count)],
                            buffer.at[pl.ds(at, count)],
                            in_sem.at[2 * k + which],
                        )
                    )
            at += count
        return result

    def span_of(i):
        return pl.ds(i * block_columns, block_columns)

    def block_copies(j):
        part = width // len(outs)
        return [
            pltpu.make_async_copy(
                res.at[pl.ds(j * part, part)], outs[j].at[q], out_sem.at[3 * j + q]
            )
            for q, res in enumerate((res_a, res_b, res_c))
        ]

    def work():
        weights = [
            pltpu.make_async_copy(w, buffer, w_sem.at[i])
            for i, (w, buffer) in enumerate(zip(weight_refs, (gate_w, up_w, down_w)))
        ]
        for copy in weights:
            copy.start()
        sizes = [entry[-1] for entry in plan[0]]

        def fetch(first_piece, last_piece):
            for choice in range(len(plan)):
                for core_value in range(2):

                    @pl.when((flags[2] == choice) & (core == core_value))
                    def _():
                        for copy in copies(choice, core_value, first_piece, last_piece):
                            copy.start()

        def needed(block):
            return next(
                k for k in range(len(sizes) + 1) if sum(sizes[:k]) >= (block + 1) * block_rows
            )

        fetch(0, needed(0))
        for copy in weights:
            copy.wait()

        def forward(first_row):
            span = pl.ds(first_row, block_rows)
            row_tokens, row_grads = tok[span, :], grd[span, :]
            pre_gate = jnp.dot(row_tokens, gate_w[...], preferred_element_type=jnp.float32)
            pre_up = jnp.dot(row_tokens, up_w[...], preferred_element_type=jnp.float32)
            hidden_back = lax.dot_general(
                row_grads, down_w[...], (((1,), (1,)), ((), ())), preferred_element_type=jnp.float32
            )
            sigmoid_gate = jax.nn.sigmoid(pre_gate)
            activated = pre_gate * sigmoid_gate
            hidden = activated * pre_up
            gate_grad = hidden_back * pre_up * sigmoid_gate * (1.0 + pre_gate * (1.0 - sigmoid_gate))
            up_grad = hidden_back * activated
            hidden_t[:, span] = hidden.T.astype(jnp.bfloat16)
            gate_up_t[pl.ds(0, hidden_width), span] = gate_grad.T.astype(jnp.bfloat16)
            gate_up_t[pl.ds(hidden_width, hidden_width), span] = up_grad.T.astype(jnp.bfloat16)

        if kind == "cold":
            fetch(needed(0), len(sizes))
            for copy in copies(0, 0, 0, len(sizes)):
                copy.wait()

            def each(i, carry):
                forward(pl.multiple_of(i * block_rows, block_rows))
                return carry

            lax.fori_loop(0, rows // block_rows, each, 0)
        else:
            arrived = 0
            for block in range(rows // block_rows):
                for copy in copies(0, 0, arrived, needed(block)):
                    copy.wait()
                arrived = needed(block)
                if block + 1 < rows // block_rows:
                    fetch(arrived, needed(block + 1))
                forward(block * block_rows)

        def products(span):
            sums = jnp.dot(gate_up_t[...], tok[:, span], preferred_element_type=jnp.float32)
            downs = jnp.dot(hidden_t[...], grd[:, span], preferred_element_type=jnp.float32)
            return sums, downs

        if kind == "cold":

            def columns(i, carry):
                span = pl.ds(pl.multiple_of(i * block_columns, block_columns), block_columns)
                sums, downs = products(span)
                sums = sums.T.astype(jnp.bfloat16)
                res_a[span, :] = sums[:, :hidden_width]
                res_b[span, :] = sums[:, hidden_width:]
                res_c[:, span] = downs.astype(jnp.bfloat16)
                return carry

            lax.fori_loop(0, column_blocks, columns, 0)
            return
        sent = 0
        for i in range(column_blocks):
            sums, downs = products(span_of(i))
            sums = sums.T.astype(jnp.bfloat16)
            res_a[span_of(i), :] = sums[:, :hidden_width]
            res_b[span_of(i), :] = sums[:, hidden_width:]
            res_c[span_of(i), :] = downs.T.astype(jnp.bfloat16)
            while (sent + 1) * (width // len(outs)) <= (i + 1) * block_columns:
                for copy in block_copies(sent):
                    copy.start()
                sent += 1
        for j in range(len(outs)):
            for copy in block_copies(j):
                copy.wait()

    @pl.when(flags[1] == 1)
    def _():
        work()

    if kind == "cold":

        @pl.when(flags[1] == 0)
        def _():
            for res in (res_a, res_b, res_c):
                res[...] = jnp.zeros_like(res)

        written = [
            pltpu.make_async_copy(res, out, out_sem.at[i])
            for i, (res, out) in enumerate(zip((res_a, res_b, res_c), outs))
        ]
        for copy in written:
            copy.start()
        done[...] = jnp.zeros_like(done)
        for copy in written:
            copy.wait()


def expert_call(kind, flags, plan, blocks, sources, weights):
    width, hidden_width = weights[0].shape
    rows = sum(entry[-1] for entry in plan[0])
    block_rows = divisor(rows, 384, 128)
    block_columns = divisor(width, 512, 128)
    bf16 = jnp.bfloat16
    scratch = [
        pltpu.VMEM((rows, width), bf16),
        pltpu.VMEM((rows, width), bf16),
        pltpu.VMEM((width, hidden_width), bf16),
        pltpu.VMEM((width, hidden_width), bf16),
        pltpu.VMEM((hidden_width, width), bf16),
        pltpu.VMEM((2 * hidden_width, rows), bf16),
        pltpu.VMEM((hidden_width, rows), bf16),
    ]
    result = pltpu.VMEM((width, hidden_width), bf16)
    if kind == "hot":
        out_shape = [jax.ShapeDtypeStruct((3, width // blocks, hidden_width), bf16)] * blocks
        scratch += [result, result, result]
    else:
        out_shape = [jax.ShapeDtypeStruct(w.shape, bf16) for w in weights]
        out_shape += [jax.ShapeDtypeStruct((8, 128), jnp.int32)]
        scratch += [result, result, pltpu.VMEM((hidden_width, width), bf16)]
    scratch += [
        pltpu.SemaphoreType.DMA((2 * len(plan[0]),)),
        pltpu.SemaphoreType.DMA((3,)),
        pltpu.SemaphoreType.DMA((3 * len(out_shape),)),
    ]
    out_specs = [ANYWHERE] * len(out_shape)
    if kind == "cold":
        out_specs[-1] = pl.BlockSpec(memory_space=pltpu.VMEM)
    kernel = functools.partial(terms_kernel, kind, plan, len(sources), block_rows, block_columns)
    return pl.pallas_call(
        kernel,
        out_shape=out_shape,
        in_specs=[pl.BlockSpec(memory_space=pltpu.SMEM)]
        + [ANYWHERE] * (len(sources) + 3),
        out_specs=out_specs,
        scratch_shapes=scratch,
        compiler_params=pltpu.CompilerParams(vmem_limit_bytes=VMEM_LIMIT),
        cost_estimate=pl.CostEstimate(
            flops=12 * rows * width * hidden_width,
            bytes_accessed=4 * rows * width + 12 * width * hidden_width,
            transcendentals=rows * hidden_width,
        ),
        name=kind + "_terms",
    )(flags, *sources, *weights)


def on_device(tokens, cotangent, gate_scale, expert_index, hot_index, w_gate, w_up, w_down):
    tok_rows, width = tokens.shape
    experts = lax.axis_size("expert")
    dp = lax.axis_size("dp")
    chips = experts // 2
    capacity = 3 * tok_rows // (2 * experts)
    if chips != 4 or dp != 4 or capacity % 8 != 0:
        return on_large_mesh(
            tokens, cotangent, gate_scale, expert_index, hot_index, w_gate, w_up, w_down
        )
    hot_expert = hot_index[0]
    me = lax.axis_index("expert")
    core, chip = me % 2, me // 2
    flat = [(i, j) for i in range(dp) for j in range(experts)]

    def place_of(i, j):
        return i * experts + j

    def swap(array):
        return lax.ppermute(array, "expert", [(j, j ^ 1) for j in range(experts)])

    def along(array, step):
        return lax.ppermute(array, "expert", [(j, j ^ (2 * step)) for j in range(experts)])

    def first_way(array):
        pairs = [(place_of(i, j), place_of(i ^ (2 if j % 2 else 1), j)) for i, j in flat]
        return lax.ppermute(array, ("dp", "expert"), pairs)

    def second_way(array):
        pairs = [(place_of(i, j), place_of(i ^ (1 if j % 2 else 2), j)) for i, j in flat]
        return lax.ppermute(array, ("dp", "expert"), pairs)

    route_grad = (gate_scale[:, None] * cotangent.astype(jnp.float32)).astype(jnp.bfloat16)
    own = jnp.where(core == 0, tokens, route_grad)
    other = jnp.where(core == 0, route_grad, tokens)
    sibling, sibling_index = swap(other), swap(expert_index)
    earlier = lax.broadcasted_iota(jnp.int32, (tok_rows, tok_rows), 1) < lax.broadcasted_iota(
        jnp.int32, (tok_rows, tok_rows), 0
    )

    def places(index):
        return jnp.sum(((index[:, None] == index[None, :]) & earlier).astype(jnp.int32), axis=1)

    index = jnp.concatenate([expert_index, sibling_index])
    place = jnp.concatenate([places(expert_index), places(sibling_index)])
    holder = jnp.concatenate([jnp.full((tok_rows,), core), jnp.full((tok_rows,), 1 - core)])
    values = jnp.concatenate([own, sibling], axis=0)
    message = 2 * capacity
    slots = lax.broadcasted_iota(jnp.int32, (message, 2 * tok_rows), 0)

    def selector(kind, step):
        target = chip ^ step
        expert = jnp.where(hot_expert // 2 == target, hot_expert, 2 * target)
        offset = 0
        if kind == "second":
            expert = expert ^ 1
        elif kind == "rest":
            expert, offset = hot_expert, capacity
        taken = (index == expert) & (place >= offset) & (place < offset + capacity)
        slot = place - offset + capacity * holder
        return ((slots == slot[None, :]) & taken[None, :]).astype(jnp.bfloat16)

    def rows(*wanted):
        return route_rows(jnp.concatenate([selector(*w) for w in wanted], axis=0), values)

    weights = (w_gate[0], w_up[0], w_down[0])
    is_owner = me == hot_expert
    owns = is_owner.astype(jnp.int32)
    zero = jnp.zeros((), jnp.int32)
    hot_flags = jnp.stack([core, owns, zero])

    unit_rows, hot_rows = 3 * message, 2 * message
    weights = (w_gate[0], w_up[0], w_down[0])
    is_owner = me == hot_expert
    owns = is_owner.astype(jnp.int32)
    zero = jnp.zeros((), jnp.int32)
    hot_flags = jnp.stack([core, owns, zero])

    def pieces(unit, first, count):
        chosen = []
        for k, mirror in enumerate((0, 2, 1, 3)):
            mine = (8 * unit + 2 * k, first)
            theirs = (8 * unit + 2 * mirror + 1, first)
            chosen.append((((mine, theirs), (theirs, mine)), count))
        return tuple(chosen)

    def listed(own, swapped):
        own_swap, side_swap, near_swap, far_swap = swapped
        pairs = zip(own, (own_swap, near_swap, side_swap, far_swap))
        return [array for pair in pairs for array in pair]

    near_unit = rows(("first", 0), ("rest", 0), ("second", 0))
    sent = {k: [rows((k, s)) for s in range(1, chips)] for k in ("first", "rest", "second")}

    near_1, side_1 = first_way(near_unit), second_way(near_unit)
    got = [along(block, s) for s, block in enumerate(sent["first"], 1)]
    first_unit = jnp.concatenate(got, axis=0)
    near_unit, near_1, side_1, first_unit, *sent["rest"] = together([
        near_unit, near_1, side_1, first_unit, *sent["rest"]
    ])
    far_1 = second_way(near_1)
    near_2, side_2 = first_way(first_unit), second_way(first_unit)
    got = [along(block, s) for s, block in enumerate(sent["rest"], 1)]
    swapped_1 = [swap(a) for a in (near_unit, side_1, near_1)]
    rest_unit = jnp.concatenate(got, axis=0)
    far_1, first_unit, near_2, side_2, rest_unit, *sent["second"] = together([
        far_1, first_unit, near_2, side_2, rest_unit, *sent["second"]
    ])
    far_2 = second_way(near_2)
    near_3, side_3 = first_way(rest_unit), second_way(rest_unit)
    got = [along(block, s) for s, block in enumerate(sent["second"], 1)]
    swapped_1.append(swap(far_1))
    swapped_2 = [swap(a) for a in (first_unit, side_2, near_2)]
    second_unit = jnp.concatenate(got, axis=0)
    far_2, rest_unit, near_3, side_3, second_unit, *swapped_1 = together(
        [far_2, rest_unit, near_3, side_3, second_unit, *swapped_1]
    )
    far_3 = second_way(near_3)
    swapped_2.append(swap(far_2))
    swapped_3 = [swap(a) for a in (rest_unit, side_3, near_3)]
    sources = listed([near_unit, near_1, side_1, far_1], swapped_1)
    far_3, second_unit = together([far_3, second_unit])
    near_4, side_4 = first_way(second_unit), second_way(second_unit)
    swapped_3.append(swap(far_3))

    sources += listed([first_unit, near_2, side_2, far_2], swapped_2)
    sources += listed([rest_unit, near_3, side_3, far_3], swapped_3)
    blocks = expert_call(
        "hot",
        hot_flags,
        (pieces(0, 0, hot_rows) + pieces(1, 0, unit_rows) + pieces(2, 0, unit_rows),),
        experts,
        sources,
        weights,
    )
    second_swap = swap(second_unit)
    near_4, side_4, second_swap, *blocks = together([near_4, side_4, second_swap, *blocks])

    first_of_chip = jnp.where(hot_expert // 2 == chip, hot_expert % 2, 0)
    cold_flags = jnp.stack([core, 1 - owns, (first_of_chip != core).astype(jnp.int32)])
    first_plan = pieces(0, 0, message)
    for k in range(chips - 1):
        first_plan += pieces(1, k * message, message)
    second_plan = pieces(0, hot_rows, message)
    for k in range(chips - 1):
        second_plan += pieces(3, k * message, message)

    def finish(owner, blocks, near_4, side_4, second_unit, second_swap, sources):
        others = sorted((j for j in range(experts) if j != owner), key=lambda j: -abs(j - owner))

        def send(j):
            return lax.ppermute(blocks[j], "expert", [(owner, j)])

        far_4 = second_way(near_4)
        near_swap, side_swap = swap(near_4), swap(side_4)
        got = [send(j) for j in others[:3]]
        (far_4,) = together([far_4], got)
        far_swap = swap(far_4)
        got += [send(j) for j in others[3:]]
        *cold, done = expert_call(
            "cold",
            cold_flags,
            (first_plan, second_plan),
            experts,
            sources
            + listed(
                [second_unit, near_4, side_4, far_4], [second_swap, side_swap, near_swap, far_swap]
            ),
            weights,
        )
        arrived = functools.reduce(jnp.add, got)
        return (*cold, jnp.where(me == owner + done[0, 0], blocks[owner], arrived))

    grad_gate, grad_up, grad_down, hot_grads = lax.switch(
        hot_expert,
        [functools.partial(finish, owner) for owner in range(experts)],
        blocks,
        near_4,
        side_4,
        second_unit,
        second_swap,
        sources,
    )
    hot_grads = jnp.transpose(hot_grads, (1, 0, 2))
    return (grad_gate[None], grad_up[None], grad_down[None], hot_grads[None])


def solution(mesh):
    placed = (
        P(("dp", "expert"), None),
        P(("dp", "expert"), None),
        P(("dp", "expert")),
        P(("dp", "expert")),
        P(),
        P("expert", None, "dp"),
        P("expert", None, "dp"),
        P("expert", "dp", None),
    )
    return jax.shard_map(
        on_device,
        mesh=mesh,
        in_specs=placed,
        out_specs=(
            P("expert", None, "dp"),
            P("expert", None, "dp"),
            P("expert", "dp", None),
            P(None, "expert", None, "dp"),
        ),
        check_vma=False,
    )
```

```python
import functools

import jax
import jax.numpy as jnp
from jax import lax
from jax.experimental import pallas as pl
from jax.experimental.pallas import tpu as pltpu
from jax.sharding import PartitionSpec as P

CONTRACT_ROWS = (((0,), (0,)), ((), ()))


def spread(block, axis, source):
    block = jnp.where(lax.axis_index(axis) == source, block, jnp.zeros_like(block))
    return lax.psum(block, axis)


def expert_terms(row_tokens, row_grads, gate_matrix, up_matrix, down_matrix):
    pre_gate = jnp.dot(row_tokens, gate_matrix, preferred_element_type=jnp.float32)
    pre_up = jnp.dot(row_tokens, up_matrix, preferred_element_type=jnp.float32)
    hidden_back = lax.dot_general(
        row_grads, down_matrix, (((1,), (1,)), ((), ())), preferred_element_type=jnp.float32
    )
    sigmoid_gate = jax.nn.sigmoid(pre_gate)
    activated = pre_gate * sigmoid_gate
    hidden = (activated * pre_up).astype(jnp.bfloat16)
    gate_grad = (
        hidden_back * pre_up * sigmoid_gate * (1.0 + pre_gate * (1.0 - sigmoid_gate))
    ).astype(jnp.bfloat16)
    up_grad = (hidden_back * activated).astype(jnp.bfloat16)
    return (hidden, gate_grad, up_grad)


def column_sum(left, right):
    return lax.dot_general(left, right, CONTRACT_ROWS, preferred_element_type=jnp.float32)


def route_rows(selector, values):
    return jnp.dot(selector, values, preferred_element_type=jnp.float32).astype(jnp.bfloat16)


def on_large_mesh(tokens, cotangent, gate_scale, expert_index, hot_index, w_gate, w_up, w_down):
    tok_rows, feature_width = tokens.shape
    experts = lax.axis_size("expert")
    capacity = 3 * tok_rows // (2 * experts)
    hot_capacity = 2 * capacity
    hot_expert = hot_index[0]
    route_grad = (gate_scale[:, None] * cotangent.astype(jnp.float32)).astype(jnp.bfloat16)
    is_hot = expert_index == hot_expert
    not_hot = jnp.logical_not(is_hot)
    owners = lax.broadcasted_iota(jnp.int32, (tok_rows, experts), 1)
    member = ((expert_index[:, None] == owners) & not_hot[:, None]).astype(jnp.int32)
    bucket_place = jnp.sum((jnp.cumsum(member, axis=0) - 1) * member, axis=1)
    slot_index = expert_index * capacity + bucket_place
    slot_grid = lax.broadcasted_iota(jnp.int32, (experts * capacity, tok_rows), 0)
    cold_map = ((slot_grid == slot_index[None, :]) & not_hot[None, :]).astype(jnp.bfloat16)
    hot_place = jnp.cumsum(is_hot.astype(jnp.int32)) - 1
    hot_grid = lax.broadcasted_iota(jnp.int32, (hot_capacity, tok_rows), 0)
    hot_map = ((hot_grid == hot_place[None, :]) & is_hot[None, :]).astype(jnp.bfloat16)
    send_tokens = route_rows(cold_map, tokens).reshape(experts, capacity, feature_width)
    send_grads = route_rows(cold_map, route_grad).reshape(experts, capacity, feature_width)
    own_hot_tokens = route_rows(hot_map, tokens)
    own_hot_grads = route_rows(hot_map, route_grad)
    arrived_tokens, arrived_grads = (
        lax.all_to_all(send_tokens, "expert", split_axis=0, concat_axis=0, tiled=True),
        lax.all_to_all(send_grads, "expert", split_axis=0, concat_axis=0, tiled=True),
    )
    cold_tokens, cold_grads, hot_tokens, hot_row_grads = (
        lax.all_gather(
            arrived_tokens.reshape(experts * capacity, feature_width), "dp", axis=0, tiled=True
        ),
        lax.all_gather(
            arrived_grads.reshape(experts * capacity, feature_width), "dp", axis=0, tiled=True
        ),
        lax.all_gather(own_hot_tokens, "dp", axis=0, tiled=True),
        lax.all_gather(own_hot_grads, "dp", axis=0, tiled=True),
    )
    shadow_gate, shadow_up, shadow_down = (
        spread(w_gate[0], "expert", hot_expert),
        spread(w_up[0], "expert", hot_expert),
        spread(w_down[0], "expert", hot_expert),
    )
    hidden, gate_grad, up_grad = expert_terms(
        cold_tokens, cold_grads, w_gate[0], w_up[0], w_down[0]
    )
    grad_gate = column_sum(cold_tokens, gate_grad).astype(jnp.bfloat16)
    grad_up = column_sum(cold_tokens, up_grad).astype(jnp.bfloat16)
    grad_down = column_sum(hidden, cold_grads).astype(jnp.bfloat16)
    hot_hidden, hot_gate_grad, hot_up_grad = expert_terms(
        hot_tokens, hot_row_grads, shadow_gate, shadow_up, shadow_down
    )
    gate_part = column_sum(hot_tokens, hot_gate_grad)
    up_part = column_sum(hot_tokens, hot_up_grad)
    down_part = column_sum(hot_row_grads, hot_hidden)
    owned_part = lax.psum_scatter(
        jnp.stack([gate_part, up_part, down_part], axis=1),
        "expert",
        scatter_dimension=0,
        tiled=True,
    )
    hot_grads = owned_part.astype(jnp.bfloat16)[None]
    return (grad_gate[None], grad_up[None], grad_down[None], hot_grads)


ANYWHERE = pl.BlockSpec(memory_space=pltpu.HBM)
VMEM_LIMIT = 56 * 2**20


def together(passed, awaited=()):
    n = len(passed)
    return pl.pallas_call(
        lambda *refs: None,
        out_shape=[jax.ShapeDtypeStruct(a.shape, a.dtype) for a in passed],
        in_specs=[pl.BlockSpec(memory_space=pl.ANY)] * (n + len(awaited)),
        out_specs=[pl.BlockSpec(memory_space=pl.ANY)] * n,
        input_output_aliases={i: i for i in range(n)},
        name="together",
    )(*passed, *awaited)


def divisor(size, most, unit):
    return max(d for d in range(unit, most + 1, unit) if size % d == 0)


def terms_kernel(kind, plan, n_sources, block_rows, block_columns, *refs):
    flags, refs = refs[0], refs[1:]
    sources, refs = refs[:n_sources], refs[n_sources:]
    weight_refs, refs = refs[:3], refs[3:]
    in_sem, w_sem, out_sem = refs[-3:]
    refs = refs[:-3]
    if kind == "cold":
        *outs, done, tok, grd, gate_w, up_w, down_w, gate_up_t, hidden_t, res_a, res_b, res_c = refs
    else:
        *outs, tok, grd, gate_w, up_w, down_w, gate_up_t, hidden_t, res_a, res_b, res_c = refs
    rows, width = tok.shape
    hidden_width = gate_w.shape[1]
    core = flags[0]
    column_blocks = width // block_columns

    def copies(choice, core_value, first_piece, last_piece):
        at, result = 0, []
        for k, (by_core, count) in enumerate(plan[choice]):
            if first_piece <= k < last_piece:
                for which, buffer in enumerate((tok, grd)):
                    source, first = by_core[core_value][which]
                    result.append(
                        pltpu.make_async_copy(
                            sources[source].at[pl.ds(first, count)],
                            buffer.at[pl.ds(at, count)],
                            in_sem.at[2 * k + which],
                        )
                    )
            at += count
        return result

    def span_of(i):
        return pl.ds(i * block_columns, block_columns)

    def block_copies(j):
        part = width // len(outs)
        return [
            pltpu.make_async_copy(
                res.at[pl.ds(j * part, part)], outs[j].at[q], out_sem.at[3 * j + q]
            )
            for q, res in enumerate((res_a, res_b, res_c))
        ]

    def work():
        weights = [
            pltpu.make_async_copy(w, buffer, w_sem.at[i])
            for i, (w, buffer) in enumerate(zip(weight_refs, (gate_w, up_w, down_w)))
        ]
        for copy in weights:
            copy.start()
        sizes = [entry[-1] for entry in plan[0]]

        def fetch(first_piece, last_piece):
            for choice in range(len(plan)):
                for core_value in range(2):

                    @pl.when((flags[2] == choice) & (core == core_value))
                    def _():
                        for copy in copies(choice, core_value, first_piece, last_piece):
                            copy.start()

        def needed(block):
            return next(
                k for k in range(len(sizes) + 1) if sum(sizes[:k]) >= (block + 1) * block_rows
            )

        fetch(0, needed(0))
        for copy in weights:
            copy.wait()

        def forward(first_row):
            span = pl.ds(first_row, block_rows)
            row_tokens, row_grads = tok[span, :], grd[span, :]
            pre_gate = jnp.dot(row_tokens, gate_w[...], preferred_element_type=jnp.float32)
            pre_up = jnp.dot(row_tokens, up_w[...], preferred_element_type=jnp.float32)
            hidden_back = lax.dot_general(
                row_grads, down_w[...], (((1,), (1,)), ((), ())), preferred_element_type=jnp.float32
            )
            sigmoid_gate = jax.nn.sigmoid(pre_gate)
            activated = pre_gate * sigmoid_gate
            hidden = activated * pre_up
            gate_grad = hidden_back * pre_up * sigmoid_gate * (1.0 + pre_gate * (1.0 - sigmoid_gate))
            up_grad = hidden_back * activated
            hidden_t[:, span] = hidden.T.astype(jnp.bfloat16)
            gate_up_t[pl.ds(0, hidden_width), span] = gate_grad.T.astype(jnp.bfloat16)
            gate_up_t[pl.ds(hidden_width, hidden_width), span] = up_grad.T.astype(jnp.bfloat16)

        if kind == "cold":
            fetch(needed(0), len(sizes))
            for copy in copies(0, 0, 0, len(sizes)):
                copy.wait()

            def each(i, carry):
                forward(pl.multiple_of(i * block_rows, block_rows))
                return carry

            lax.fori_loop(0, rows // block_rows, each, 0)
        else:
            arrived = 0
            for block in range(rows // block_rows):
                for copy in copies(0, 0, arrived, needed(block)):
                    copy.wait()
                arrived = needed(block)
                if block == 0:
                    fetch(arrived, len(sizes))
                forward(block * block_rows)

        def products(span):
            sums = jnp.dot(gate_up_t[...], tok[:, span], preferred_element_type=jnp.float32)
            downs = jnp.dot(hidden_t[...], grd[:, span], preferred_element_type=jnp.float32)
            return sums, downs

        if kind == "cold":

            def columns(i, carry):
                span = pl.ds(pl.multiple_of(i * block_columns, block_columns), block_columns)
                sums, downs = products(span)
                sums = sums.T.astype(jnp.bfloat16)
                res_a[span, :] = sums[:, :hidden_width]
                res_b[span, :] = sums[:, hidden_width:]
                res_c[:, span] = downs.astype(jnp.bfloat16)
                return carry

            lax.fori_loop(0, column_blocks, columns, 0)
            return
        sent = 0
        for i in range(column_blocks):
            sums, downs = products(span_of(i))
            sums = sums.T.astype(jnp.bfloat16)
            res_a[span_of(i), :] = sums[:, :hidden_width]
            res_b[span_of(i), :] = sums[:, hidden_width:]
            res_c[span_of(i), :] = downs.T.astype(jnp.bfloat16)
            while (sent + 1) * (width // len(outs)) <= (i + 1) * block_columns:
                for copy in block_copies(sent):
                    copy.start()
                sent += 1
        for j in range(len(outs)):
            for copy in block_copies(j):
                copy.wait()

    @pl.when(flags[1] == 1)
    def _():
        work()

    if kind == "cold":

        @pl.when(flags[1] == 0)
        def _():
            for res in (res_a, res_b, res_c):
                res[...] = jnp.zeros_like(res)

        written = [
            pltpu.make_async_copy(res, out, out_sem.at[i])
            for i, (res, out) in enumerate(zip((res_a, res_b, res_c), outs))
        ]
        for copy in written:
            copy.start()
        done[...] = jnp.zeros_like(done)
        for copy in written:
            copy.wait()


def expert_call(kind, flags, plan, blocks, sources, weights):
    width, hidden_width = weights[0].shape
    rows = sum(entry[-1] for entry in plan[0])
    block_rows = divisor(rows, 384 if kind == "hot" else 128, 128)
    block_columns = divisor(width, 512 if kind == "hot" else 256, 128)
    bf16 = jnp.bfloat16
    scratch = [
        pltpu.VMEM((rows, width), bf16),
        pltpu.VMEM((rows, width), bf16),
        pltpu.VMEM((width, hidden_width), bf16),
        pltpu.VMEM((width, hidden_width), bf16),
        pltpu.VMEM((hidden_width, width), bf16),
        pltpu.VMEM((2 * hidden_width, rows), bf16),
        pltpu.VMEM((hidden_width, rows), bf16),
    ]
    result = pltpu.VMEM((width, hidden_width), bf16)
    if kind == "hot":
        out_shape = [jax.ShapeDtypeStruct((3, width // blocks, hidden_width), bf16)] * blocks
        scratch += [result, result, result]
    else:
        out_shape = [jax.ShapeDtypeStruct(w.shape, bf16) for w in weights]
        out_shape += [jax.ShapeDtypeStruct((8, 128), jnp.int32)]
        scratch += [result, result, pltpu.VMEM((hidden_width, width), bf16)]
    scratch += [
        pltpu.SemaphoreType.DMA((2 * len(plan[0]),)),
        pltpu.SemaphoreType.DMA((3,)),
        pltpu.SemaphoreType.DMA((3 * len(out_shape),)),
    ]
    out_specs = [ANYWHERE] * len(out_shape)
    if kind == "cold":
        out_specs[-1] = pl.BlockSpec(memory_space=pltpu.VMEM)
    kernel = functools.partial(terms_kernel, kind, plan, len(sources), block_rows, block_columns)
    return pl.pallas_call(
        kernel,
        out_shape=out_shape,
        in_specs=[pl.BlockSpec(memory_space=pltpu.SMEM)]
        + [ANYWHERE] * (len(sources) + 3),
        out_specs=out_specs,
        scratch_shapes=scratch,
        compiler_params=pltpu.CompilerParams(vmem_limit_bytes=VMEM_LIMIT),
        cost_estimate=pl.CostEstimate(
            flops=12 * rows * width * hidden_width,
            bytes_accessed=4 * rows * width + 12 * width * hidden_width,
            transcendentals=rows * hidden_width,
        ),
        name=kind + "_terms",
    )(flags, *sources, *weights)


def on_device(tokens, cotangent, gate_scale, expert_index, hot_index, w_gate, w_up, w_down):
    tok_rows, width = tokens.shape
    experts = lax.axis_size("expert")
    dp = lax.axis_size("dp")
    chips = experts // 2
    capacity = 3 * tok_rows // (2 * experts)
    if chips != 4 or dp != 4 or capacity % 8 != 0:
        return on_large_mesh(
            tokens, cotangent, gate_scale, expert_index, hot_index, w_gate, w_up, w_down
        )
    hot_expert = hot_index[0]
    me = lax.axis_index("expert")
    core, chip = me % 2, me // 2
    flat = [(i, j) for i in range(dp) for j in range(experts)]

    def place_of(i, j):
        return i * experts + j

    def swap(array):
        return lax.ppermute(array, "expert", [(j, j ^ 1) for j in range(experts)])

    def along(array, step):
        return lax.ppermute(array, "expert", [(j, j ^ (2 * step)) for j in range(experts)])

    def first_way(array):
        pairs = [(place_of(i, j), place_of(i ^ (2 if j % 2 else 1), j)) for i, j in flat]
        return lax.ppermute(array, ("dp", "expert"), pairs)

    def second_way(array):
        pairs = [(place_of(i, j), place_of(i ^ (1 if j % 2 else 2), j)) for i, j in flat]
        return lax.ppermute(array, ("dp", "expert"), pairs)

    route_grad = (gate_scale[:, None] * cotangent.astype(jnp.float32)).astype(jnp.bfloat16)
    own = jnp.where(core == 0, tokens, route_grad)
    other = jnp.where(core == 0, route_grad, tokens)
    sibling, sibling_index = swap(other), swap(expert_index)
    earlier = lax.broadcasted_iota(jnp.int32, (tok_rows, tok_rows), 1) < lax.broadcasted_iota(
        jnp.int32, (tok_rows, tok_rows), 0
    )

    def places(index):
        return jnp.sum(((index[:, None] == index[None, :]) & earlier).astype(jnp.int32), axis=1)

    index = jnp.concatenate([expert_index, sibling_index])
    place = jnp.concatenate([places(expert_index), places(sibling_index)])
    holder = jnp.concatenate([jnp.full((tok_rows,), core), jnp.full((tok_rows,), 1 - core)])
    values = jnp.concatenate([own, sibling], axis=0)
    message = 2 * capacity
    slots = lax.broadcasted_iota(jnp.int32, (message, 2 * tok_rows), 0)

    def selector(kind, step):
        target = chip ^ step
        expert = jnp.where(hot_expert // 2 == target, hot_expert, 2 * target)
        offset = 0
        if kind == "second":
            expert = expert ^ 1
        elif kind == "rest":
            expert, offset = hot_expert, capacity
        taken = (index == expert) & (place >= offset) & (place < offset + capacity)
        slot = place - offset + capacity * holder
        return ((slots == slot[None, :]) & taken[None, :]).astype(jnp.bfloat16)

    def rows(*wanted):
        return route_rows(jnp.concatenate([selector(*w) for w in wanted], axis=0), values)

    weights = (w_gate[0], w_up[0], w_down[0])
    is_owner = me == hot_expert
    owns = is_owner.astype(jnp.int32)
    zero = jnp.zeros((), jnp.int32)
    hot_flags = jnp.stack([core, owns, zero])

    unit_rows, hot_rows = 3 * message, 2 * message
    weights = (w_gate[0], w_up[0], w_down[0])
    is_owner = me == hot_expert
    owns = is_owner.astype(jnp.int32)
    zero = jnp.zeros((), jnp.int32)
    hot_flags = jnp.stack([core, owns, zero])

    def pieces(unit, first, count):
        chosen = []
        for k, mirror in enumerate((0, 2, 1, 3)):
            mine = (8 * unit + 2 * k, first)
            theirs = (8 * unit + 2 * mirror + 1, first)
            chosen.append((((mine, theirs), (theirs, mine)), count))
        return tuple(chosen)

    def listed(own, swapped):
        own_swap, side_swap, near_swap, far_swap = swapped
        pairs = zip(own, (own_swap, near_swap, side_swap, far_swap))
        return [array for pair in pairs for array in pair]

    near_unit = rows(("first", 0), ("rest", 0))
    sent = {k: [rows((k, s)) for s in range(1, chips)] for k in ("first", "rest", "second")}

    own_second = rows(("second", 0))

    near_1, side_1 = first_way(near_unit), second_way(near_unit)
    got = [along(block, s) for s, block in enumerate(sent["first"], 1)]
    first_unit = jnp.concatenate(got, axis=0)
    near_unit, near_1, side_1, first_unit, *held = together(
        [near_unit, near_1, side_1, first_unit, *sent["rest"], *sent["second"]]
    )
    sent["rest"], sent["second"] = held[: chips - 1], held[chips - 1 :]
    far_1 = second_way(near_1)
    near_2, side_2 = first_way(first_unit), second_way(first_unit)
    got = [along(block, s) for s, block in enumerate(sent["rest"], 1)]
    swapped_1 = [swap(a) for a in (near_unit, side_1, near_1)]
    rest_unit = jnp.concatenate(got, axis=0)
    far_1, first_unit, near_2, side_2, rest_unit, *sent["second"] = together([
        far_1, first_unit, near_2, side_2, rest_unit, *sent["second"]
    ])
    far_2 = second_way(near_2)
    near_3, side_3 = first_way(rest_unit), second_way(rest_unit)
    got = [along(block, s) for s, block in enumerate(sent["second"], 1)]
    swapped_1.append(swap(far_1))
    swapped_2 = [swap(a) for a in (first_unit, side_2, near_2)]
    second_unit = jnp.concatenate([own_second] + got, axis=0)
    far_2, rest_unit, near_3, side_3, second_unit, *swapped_1 = together(
        [far_2, rest_unit, near_3, side_3, second_unit, *swapped_1]
    )
    far_3 = second_way(near_3)
    swapped_2.append(swap(far_2))
    swapped_3 = [swap(a) for a in (rest_unit, side_3, near_3)]
    sources = listed([near_unit, near_1, side_1, far_1], swapped_1)
    far_3, second_unit = together([far_3, second_unit])
    near_4, side_4 = first_way(second_unit), second_way(second_unit)
    swapped_3.append(swap(far_3))

    sources += listed([first_unit, near_2, side_2, far_2], swapped_2)
    sources += listed([rest_unit, near_3, side_3, far_3], swapped_3)
    blocks = expert_call(
        "hot",
        hot_flags,
        (pieces(0, 0, hot_rows) + pieces(1, 0, unit_rows) + pieces(2, 0, unit_rows),),
        experts,
        sources,
        weights,
    )
    second_swap = swap(second_unit)
    near_4, side_4, second_swap, *blocks = together([near_4, side_4, second_swap, *blocks])

    first_of_chip = jnp.where(hot_expert // 2 == chip, hot_expert % 2, 0)
    cold_flags = jnp.stack([core, 1 - owns, (first_of_chip != core).astype(jnp.int32)])
    first_plan = pieces(0, 0, message)
    for k in range(chips - 1):
        first_plan += pieces(1, k * message, message)
    second_plan = ()
    for k in range(chips):
        second_plan += pieces(3, k * message, message)

    def finish(owner, blocks, near_4, side_4, second_unit, second_swap, sources):
        others = sorted((j for j in range(experts) if j != owner), key=lambda j: -abs(j - owner))

        def send(j):
            return lax.ppermute(blocks[j], "expert", [(owner, j)])

        far_4 = second_way(near_4)
        near_swap, side_swap = swap(near_4), swap(side_4)
        got = [send(j) for j in others[:3]]
        (far_4,) = together([far_4], got)
        far_swap = swap(far_4)
        got += [send(j) for j in others[3:]]
        *cold, done = expert_call(
            "cold",
            cold_flags,
            (first_plan, second_plan),
            experts,
            sources
            + listed(
                [second_unit, near_4, side_4, far_4], [second_swap, side_swap, near_swap, far_swap]
            ),
            weights,
        )
        arrived = functools.reduce(jnp.add, got)
        return (*cold, jnp.where(me == owner + done[0, 0], blocks[owner], arrived))

    grad_gate, grad_up, grad_down, hot_grads = lax.switch(
        hot_expert,
        [functools.partial(finish, owner) for owner in range(experts)],
        blocks,
        near_4,
        side_4,
        second_unit,
        second_swap,
        sources,
    )
    hot_grads = jnp.transpose(hot_grads, (1, 0, 2))
    return (grad_gate[None], grad_up[None], grad_down[None], hot_grads[None])


def solution(mesh):
    placed = (
        P(("dp", "expert"), None),
        P(("dp", "expert"), None),
        P(("dp", "expert")),
        P(("dp", "expert")),
        P(),
        P("expert", None, "dp"),
        P("expert", None, "dp"),
        P("expert", "dp", None),
    )
    return jax.shard_map(
        on_device,
        mesh=mesh,
        in_specs=placed,
        out_specs=(
            P("expert", None, "dp"),
            P("expert", None, "dp"),
            P("expert", "dp", None),
            P(None, "expert", None, "dp"),
        ),
        check_vma=False,
    )
```

```python
import functools

import jax
import jax.numpy as jnp
from jax import lax
from jax.experimental import pallas as pl
from jax.experimental.pallas import tpu as pltpu
from jax.sharding import PartitionSpec as P

CONTRACT_ROWS = (((0,), (0,)), ((), ()))


def spread(block, axis, source):
    block = jnp.where(lax.axis_index(axis) == source, block, jnp.zeros_like(block))
    return lax.psum(block, axis)


def expert_terms(row_tokens, row_grads, gate_matrix, up_matrix, down_matrix):
    pre_gate = jnp.dot(row_tokens, gate_matrix, preferred_element_type=jnp.float32)
    pre_up = jnp.dot(row_tokens, up_matrix, preferred_element_type=jnp.float32)
    hidden_back = lax.dot_general(
        row_grads, down_matrix, (((1,), (1,)), ((), ())), preferred_element_type=jnp.float32
    )
    sigmoid_gate = jax.nn.sigmoid(pre_gate)
    activated = pre_gate * sigmoid_gate
    hidden = (activated * pre_up).astype(jnp.bfloat16)
    gate_grad = (
        hidden_back * pre_up * sigmoid_gate * (1.0 + pre_gate * (1.0 - sigmoid_gate))
    ).astype(jnp.bfloat16)
    up_grad = (hidden_back * activated).astype(jnp.bfloat16)
    return (hidden, gate_grad, up_grad)


def column_sum(left, right):
    return lax.dot_general(left, right, CONTRACT_ROWS, preferred_element_type=jnp.float32)


def route_rows(selector, values):
    return jnp.dot(selector, values, preferred_element_type=jnp.float32).astype(jnp.bfloat16)


def on_large_mesh(tokens, cotangent, gate_scale, expert_index, hot_index, w_gate, w_up, w_down):
    tok_rows, feature_width = tokens.shape
    experts = lax.axis_size("expert")
    capacity = 3 * tok_rows // (2 * experts)
    hot_capacity = 2 * capacity
    hot_expert = hot_index[0]
    route_grad = (gate_scale[:, None] * cotangent.astype(jnp.float32)).astype(jnp.bfloat16)
    is_hot = expert_index == hot_expert
    not_hot = jnp.logical_not(is_hot)
    owners = lax.broadcasted_iota(jnp.int32, (tok_rows, experts), 1)
    member = ((expert_index[:, None] == owners) & not_hot[:, None]).astype(jnp.int32)
    bucket_place = jnp.sum((jnp.cumsum(member, axis=0) - 1) * member, axis=1)
    slot_index = expert_index * capacity + bucket_place
    slot_grid = lax.broadcasted_iota(jnp.int32, (experts * capacity, tok_rows), 0)
    cold_map = ((slot_grid == slot_index[None, :]) & not_hot[None, :]).astype(jnp.bfloat16)
    hot_place = jnp.cumsum(is_hot.astype(jnp.int32)) - 1
    hot_grid = lax.broadcasted_iota(jnp.int32, (hot_capacity, tok_rows), 0)
    hot_map = ((hot_grid == hot_place[None, :]) & is_hot[None, :]).astype(jnp.bfloat16)
    send_tokens = route_rows(cold_map, tokens).reshape(experts, capacity, feature_width)
    send_grads = route_rows(cold_map, route_grad).reshape(experts, capacity, feature_width)
    own_hot_tokens = route_rows(hot_map, tokens)
    own_hot_grads = route_rows(hot_map, route_grad)
    arrived_tokens, arrived_grads = (
        lax.all_to_all(send_tokens, "expert", split_axis=0, concat_axis=0, tiled=True),
        lax.all_to_all(send_grads, "expert", split_axis=0, concat_axis=0, tiled=True),
    )
    cold_tokens, cold_grads, hot_tokens, hot_row_grads = (
        lax.all_gather(
            arrived_tokens.reshape(experts * capacity, feature_width), "dp", axis=0, tiled=True
        ),
        lax.all_gather(
            arrived_grads.reshape(experts * capacity, feature_width), "dp", axis=0, tiled=True
        ),
        lax.all_gather(own_hot_tokens, "dp", axis=0, tiled=True),
        lax.all_gather(own_hot_grads, "dp", axis=0, tiled=True),
    )
    shadow_gate, shadow_up, shadow_down = (
        spread(w_gate[0], "expert", hot_expert),
        spread(w_up[0], "expert", hot_expert),
        spread(w_down[0], "expert", hot_expert),
    )
    hidden, gate_grad, up_grad = expert_terms(
        cold_tokens, cold_grads, w_gate[0], w_up[0], w_down[0]
    )
    grad_gate = column_sum(cold_tokens, gate_grad).astype(jnp.bfloat16)
    grad_up = column_sum(cold_tokens, up_grad).astype(jnp.bfloat16)
    grad_down = column_sum(hidden, cold_grads).astype(jnp.bfloat16)
    hot_hidden, hot_gate_grad, hot_up_grad = expert_terms(
        hot_tokens, hot_row_grads, shadow_gate, shadow_up, shadow_down
    )
    gate_part = column_sum(hot_tokens, hot_gate_grad)
    up_part = column_sum(hot_tokens, hot_up_grad)
    down_part = column_sum(hot_row_grads, hot_hidden)
    owned_part = lax.psum_scatter(
        jnp.stack([gate_part, up_part, down_part], axis=1),
        "expert",
        scatter_dimension=0,
        tiled=True,
    )
    hot_grads = owned_part.astype(jnp.bfloat16)[None]
    return (grad_gate[None], grad_up[None], grad_down[None], hot_grads)


ANYWHERE = pl.BlockSpec(memory_space=pltpu.HBM)
VMEM_LIMIT = 56 * 2**20


def together(passed, awaited=()):
    n = len(passed)
    return pl.pallas_call(
        lambda *refs: None,
        out_shape=[jax.ShapeDtypeStruct(a.shape, a.dtype) for a in passed],
        in_specs=[pl.BlockSpec(memory_space=pl.ANY)] * (n + len(awaited)),
        out_specs=[pl.BlockSpec(memory_space=pl.ANY)] * n,
        input_output_aliases={i: i for i in range(n)},
        name="together",
    )(*passed, *awaited)


def divisor(size, most, unit):
    return max(d for d in range(unit, most + 1, unit) if size % d == 0)


def terms_kernel(kind, plan, n_sources, block_rows, block_columns, *refs):
    flags, refs = refs[0], refs[1:]
    sources, refs = refs[:n_sources], refs[n_sources:]
    weight_refs, refs = refs[:3], refs[3:]
    in_sem, w_sem, out_sem = refs[-3:]
    refs = refs[:-3]
    if kind == "cold":
        *outs, done, tok, grd, gate_w, up_w, down_w, gate_up_t, hidden_t, res_a, res_b, res_c = refs
    else:
        *outs, tok, grd, gate_w, up_w, down_w, gate_up_t, hidden_t, res_a, res_b, res_c = refs
    rows, width = tok.shape
    hidden_width = gate_w.shape[1]
    core = flags[0]
    column_blocks = width // block_columns

    def copies(choice, core_value, first_piece, last_piece):
        at, result = 0, []
        for k, (by_core, count) in enumerate(plan[choice]):
            if first_piece <= k < last_piece:
                for which, buffer in enumerate((tok, grd)):
                    source, first = by_core[core_value][which]
                    result.append(
                        pltpu.make_async_copy(
                            sources[source].at[pl.ds(first, count)],
                            buffer.at[pl.ds(at, count)],
                            in_sem.at[2 * k + which],
                        )
                    )
            at += count
        return result

    def span_of(i):
        return pl.ds(i * block_columns, block_columns)

    def block_copies(j, core_value):
        part = width // (2 * outs[0].shape[0])
        return [
            pltpu.make_async_copy(
                res.at[pl.ds(j * part, part)],
                outs[int(j % 2 != core_value)].at[j // 2, q],
                out_sem.at[3 * j + q],
            )
            for q, res in enumerate((res_a, res_b, res_c))
        ]

    def work():
        weights = [
            pltpu.make_async_copy(w, buffer, w_sem.at[i])
            for i, (w, buffer) in enumerate(zip(weight_refs, (gate_w, up_w, down_w)))
        ]
        for copy in weights:
            copy.start()
        sizes = [entry[-1] for entry in plan[0]]

        def fetch(first_piece, last_piece):
            for choice in range(len(plan)):
                for core_value in range(2):

                    @pl.when((flags[2] == choice) & (core == core_value))
                    def _():
                        for copy in copies(choice, core_value, first_piece, last_piece):
                            copy.start()

        def needed(block):
            return next(
                k for k in range(len(sizes) + 1) if sum(sizes[:k]) >= (block + 1) * block_rows
            )

        fetch(0, needed(0))
        for copy in weights:
            copy.wait()

        def forward(first_row):
            span = pl.ds(first_row, block_rows)
            row_tokens, row_grads = tok[span, :], grd[span, :]
            pre_gate = jnp.dot(row_tokens, gate_w[...], preferred_element_type=jnp.float32)
            pre_up = jnp.dot(row_tokens, up_w[...], preferred_element_type=jnp.float32)
            hidden_back = lax.dot_general(
                row_grads, down_w[...], (((1,), (1,)), ((), ())), preferred_element_type=jnp.float32
            )
            sigmoid_gate = jax.nn.sigmoid(pre_gate)
            activated = pre_gate * sigmoid_gate
            hidden = activated * pre_up
            gate_grad = hidden_back * pre_up * sigmoid_gate * (1.0 + pre_gate * (1.0 - sigmoid_gate))
            up_grad = hidden_back * activated
            hidden_t[:, span] = hidden.T.astype(jnp.bfloat16)
            gate_up_t[pl.ds(0, hidden_width), span] = gate_grad.T.astype(jnp.bfloat16)
            gate_up_t[pl.ds(hidden_width, hidden_width), span] = up_grad.T.astype(jnp.bfloat16)

        if kind == "cold":
            fetch(needed(0), len(sizes))
            for copy in copies(0, 0, 0, len(sizes)):
                copy.wait()

            def each(i, carry):
                forward(pl.multiple_of(i * block_rows, block_rows))
                return carry

            lax.fori_loop(0, rows // block_rows, each, 0)
        else:
            arrived = 0
            for block in range(rows // block_rows):
                for copy in copies(0, 0, arrived, needed(block)):
                    copy.wait()
                arrived = needed(block)
                if block == 0:
                    fetch(arrived, len(sizes))
                forward(block * block_rows)

        def products(span):
            sums = jnp.dot(gate_up_t[...], tok[:, span], preferred_element_type=jnp.float32)
            downs = jnp.dot(hidden_t[...], grd[:, span], preferred_element_type=jnp.float32)
            return sums, downs

        if kind == "cold":

            def columns(i, carry):
                span = pl.ds(pl.multiple_of(i * block_columns, block_columns), block_columns)
                sums, downs = products(span)
                sums = sums.T.astype(jnp.bfloat16)
                res_a[span, :] = sums[:, :hidden_width]
                res_b[span, :] = sums[:, hidden_width:]
                res_c[:, span] = downs.astype(jnp.bfloat16)
                return carry

            lax.fori_loop(0, column_blocks, columns, 0)
            return
        sent, blocks = 0, 2 * outs[0].shape[0]
        for i in range(column_blocks):
            sums, downs = products(span_of(i))
            sums = sums.T.astype(jnp.bfloat16)
            res_a[span_of(i), :] = sums[:, :hidden_width]
            res_b[span_of(i), :] = sums[:, hidden_width:]
            res_c[span_of(i), :] = downs.T.astype(jnp.bfloat16)
            ready = (i + 1) * block_columns * blocks // width
            for core_value in range(2):

                @pl.when(core == core_value)
                def _():
                    for j in range(sent, ready):
                        for copy in block_copies(j, core_value):
                            copy.start()

            sent = ready
        for j in range(blocks):
            for copy in block_copies(j, 0):
                copy.wait()

    @pl.when(flags[1] == 1)
    def _():
        work()

    if kind == "cold":

        @pl.when(flags[1] == 0)
        def _():
            for res in (res_a, res_b, res_c):
                res[...] = jnp.zeros_like(res)

        written = [
            pltpu.make_async_copy(res, out, out_sem.at[i])
            for i, (res, out) in enumerate(zip((res_a, res_b, res_c), outs))
        ]
        for copy in written:
            copy.start()
        done[...] = jnp.zeros_like(done)
        for copy in written:
            copy.wait()


def expert_call(kind, flags, plan, blocks, sources, weights):
    width, hidden_width = weights[0].shape
    rows = sum(entry[-1] for entry in plan[0])
    block_rows = divisor(rows, 384 if kind == "hot" else 128, 128)
    block_columns = divisor(width, 512 if kind == "hot" else 256, 128)
    bf16 = jnp.bfloat16
    scratch = [
        pltpu.VMEM((rows, width), bf16),
        pltpu.VMEM((rows, width), bf16),
        pltpu.VMEM((width, hidden_width), bf16),
        pltpu.VMEM((width, hidden_width), bf16),
        pltpu.VMEM((hidden_width, width), bf16),
        pltpu.VMEM((2 * hidden_width, rows), bf16),
        pltpu.VMEM((hidden_width, rows), bf16),
    ]
    result = pltpu.VMEM((width, hidden_width), bf16)
    if kind == "hot":
        chips = blocks // 2
        out_shape = [
            jax.ShapeDtypeStruct((chips, 3, width // blocks, hidden_width), bf16)
        ] * 2
        scratch += [result, result, result]
    else:
        out_shape = [jax.ShapeDtypeStruct(w.shape, bf16) for w in weights]
        out_shape += [jax.ShapeDtypeStruct((8, 128), jnp.int32)]
        scratch += [result, result, pltpu.VMEM((hidden_width, width), bf16)]
    scratch += [
        pltpu.SemaphoreType.DMA((2 * len(plan[0]),)),
        pltpu.SemaphoreType.DMA((3,)),
        pltpu.SemaphoreType.DMA((3 * blocks,)),
    ]
    out_specs = [ANYWHERE] * len(out_shape)
    if kind == "cold":
        out_specs[-1] = pl.BlockSpec(memory_space=pltpu.VMEM)
    kernel = functools.partial(terms_kernel, kind, plan, len(sources), block_rows, block_columns)
    return pl.pallas_call(
        kernel,
        out_shape=out_shape,
        in_specs=[pl.BlockSpec(memory_space=pltpu.SMEM)]
        + [ANYWHERE] * (len(sources) + 3),
        out_specs=out_specs,
        scratch_shapes=scratch,
        compiler_params=pltpu.CompilerParams(vmem_limit_bytes=VMEM_LIMIT),
        cost_estimate=pl.CostEstimate(
            flops=12 * rows * width * hidden_width,
            bytes_accessed=4 * rows * width + 12 * width * hidden_width,
            transcendentals=rows * hidden_width,
        ),
        name=kind + "_terms",
    )(flags, *sources, *weights)


def on_device(tokens, cotangent, gate_scale, expert_index, hot_index, w_gate, w_up, w_down):
    tok_rows, width = tokens.shape
    experts = lax.axis_size("expert")
    dp = lax.axis_size("dp")
    chips = experts // 2
    capacity = 3 * tok_rows // (2 * experts)
    if chips != 4 or dp != 4 or capacity % 8 != 0:
        return on_large_mesh(
            tokens, cotangent, gate_scale, expert_index, hot_index, w_gate, w_up, w_down
        )
    hot_expert = hot_index[0]
    me = lax.axis_index("expert")
    core, chip = me % 2, me // 2
    flat = [(i, j) for i in range(dp) for j in range(experts)]

    def place_of(i, j):
        return i * experts + j

    def swap(array):
        return lax.ppermute(array, "expert", [(j, j ^ 1) for j in range(experts)])

    def along(array, step):
        return lax.ppermute(array, "expert", [(j, j ^ (2 * step)) for j in range(experts)])

    def first_way(array):
        pairs = [(place_of(i, j), place_of(i ^ (2 if j % 2 else 1), j)) for i, j in flat]
        return lax.ppermute(array, ("dp", "expert"), pairs)

    def second_way(array):
        pairs = [(place_of(i, j), place_of(i ^ (1 if j % 2 else 2), j)) for i, j in flat]
        return lax.ppermute(array, ("dp", "expert"), pairs)

    route_grad = (gate_scale[:, None] * cotangent.astype(jnp.float32)).astype(jnp.bfloat16)
    own = jnp.where(core == 0, tokens, route_grad)
    other = jnp.where(core == 0, route_grad, tokens)
    sibling, sibling_index = swap(other), swap(expert_index)
    earlier = lax.broadcasted_iota(jnp.int32, (tok_rows, tok_rows), 1) < lax.broadcasted_iota(
        jnp.int32, (tok_rows, tok_rows), 0
    )

    def places(index):
        return jnp.sum(((index[:, None] == index[None, :]) & earlier).astype(jnp.int32), axis=1)

    index = jnp.concatenate([expert_index, sibling_index])
    place = jnp.concatenate([places(expert_index), places(sibling_index)])
    holder = jnp.concatenate([jnp.full((tok_rows,), core), jnp.full((tok_rows,), 1 - core)])
    values = jnp.concatenate([own, sibling], axis=0)
    message = 2 * capacity
    slots = lax.broadcasted_iota(jnp.int32, (message, 2 * tok_rows), 0)

    def selector(kind, step):
        target = chip ^ step
        expert = jnp.where(hot_expert // 2 == target, hot_expert, 2 * target)
        offset = 0
        if kind == "second":
            expert = expert ^ 1
        elif kind == "rest":
            expert, offset = hot_expert, capacity
        taken = (index == expert) & (place >= offset) & (place < offset + capacity)
        slot = place - offset + capacity * holder
        return ((slots == slot[None, :]) & taken[None, :]).astype(jnp.bfloat16)

    def rows(*wanted):
        return route_rows(jnp.concatenate([selector(*w) for w in wanted], axis=0), values)

    weights = (w_gate[0], w_up[0], w_down[0])
    is_owner = me == hot_expert
    owns = is_owner.astype(jnp.int32)
    zero = jnp.zeros((), jnp.int32)
    hot_flags = jnp.stack([core, owns, zero])

    unit_rows, hot_rows = 3 * message, 2 * message
    weights = (w_gate[0], w_up[0], w_down[0])
    is_owner = me == hot_expert
    owns = is_owner.astype(jnp.int32)
    zero = jnp.zeros((), jnp.int32)
    hot_flags = jnp.stack([core, owns, zero])

    def pieces(unit, first, count):
        chosen = []
        for k, mirror in enumerate((0, 2, 1, 3)):
            mine = (8 * unit + 2 * k, first)
            theirs = (8 * unit + 2 * mirror + 1, first)
            chosen.append((((mine, theirs), (theirs, mine)), count))
        return tuple(chosen)

    def listed(own, swapped):
        own_swap, side_swap, near_swap, far_swap = swapped
        pairs = zip(own, (own_swap, near_swap, side_swap, far_swap))
        return [array for pair in pairs for array in pair]

    near_unit = rows(("first", 0), ("rest", 0))
    sent = {k: [rows((k, s)) for s in range(1, chips)] for k in ("first", "rest", "second")}

    own_second = rows(("second", 0))

    near_1, side_1 = first_way(near_unit), second_way(near_unit)
    got = [along(block, s) for s, block in enumerate(sent["first"], 1)]
    first_unit = jnp.concatenate(got, axis=0)
    near_unit, near_1, side_1, first_unit, *held = together(
        [near_unit, near_1, side_1, first_unit, *sent["rest"], *sent["second"]]
    )
    sent["rest"], sent["second"] = held[: chips - 1], held[chips - 1 :]
    far_1 = second_way(near_1)
    near_2, side_2 = first_way(first_unit), second_way(first_unit)
    got = [along(block, s) for s, block in enumerate(sent["rest"], 1)]
    swapped_1 = [swap(a) for a in (near_unit, side_1, near_1)]
    rest_unit = jnp.concatenate(got, axis=0)
    far_1, first_unit, near_2, side_2, rest_unit, *sent["second"] = together([
        far_1, first_unit, near_2, side_2, rest_unit, *sent["second"]
    ])
    far_2 = second_way(near_2)
    near_3, side_3 = first_way(rest_unit), second_way(rest_unit)
    got = [along(block, s) for s, block in enumerate(sent["second"], 1)]
    swapped_1.append(swap(far_1))
    swapped_2 = [swap(a) for a in (first_unit, side_2, near_2)]
    second_unit = jnp.concatenate([own_second] + got, axis=0)
    far_2, rest_unit, near_3, side_3, second_unit, *swapped_1 = together(
        [far_2, rest_unit, near_3, side_3, second_unit, *swapped_1]
    )
    far_3 = second_way(near_3)
    swapped_2.append(swap(far_2))
    swapped_3 = [swap(a) for a in (rest_unit, side_3, near_3)]
    sources = listed([near_unit, near_1, side_1, far_1], swapped_1)
    far_3, second_unit = together([far_3, second_unit])
    near_4, side_4 = first_way(second_unit), second_way(second_unit)
    swapped_3.append(swap(far_3))

    sources += listed([first_unit, near_2, side_2, far_2], swapped_2)
    sources += listed([rest_unit, near_3, side_3, far_3], swapped_3)
    kept, given = expert_call(
        "hot",
        hot_flags,
        (pieces(0, 0, hot_rows) + pieces(1, 0, unit_rows) + pieces(2, 0, unit_rows),),
        experts,
        sources,
        weights,
    )
    second_swap = swap(second_unit)
    near_4, side_4, second_swap, kept, given = together([near_4, side_4, second_swap, kept, given])
    taken = swap(given)

    first_of_chip = jnp.where(hot_expert // 2 == chip, hot_expert % 2, 0)
    cold_flags = jnp.stack([core, 1 - owns, (first_of_chip != core).astype(jnp.int32)])
    first_plan = pieces(0, 0, message)
    for k in range(chips - 1):
        first_plan += pieces(1, k * message, message)
    second_plan = ()
    for k in range(chips):
        second_plan += pieces(3, k * message, message)

    def finish(owner, kept, taken, near_4, side_4, second_unit, second_swap, sources):
        others = sorted((z for z in range(chips) if z != owner), key=lambda z: -abs(z - owner))
        blocks = jnp.where(is_owner, kept, taken)

        def send(z):
            pairs = [(2 * owner + c, 2 * z + c) for c in range(2)]
            return lax.ppermute(blocks[z], "expert", pairs)

        far_4 = second_way(near_4)
        near_swap, side_swap = swap(near_4), swap(side_4)
        got = [send(others[0])]
        (far_4,) = together([far_4], got)
        far_swap = swap(far_4)
        got += [send(z) for z in others[1:]]
        *cold, done = expert_call(
            "cold",
            cold_flags,
            (first_plan, second_plan),
            experts,
            sources
            + listed(
                [second_unit, near_4, side_4, far_4], [second_swap, side_swap, near_swap, far_swap]
            ),
            weights,
        )
        arrived = functools.reduce(jnp.add, got)
        return (*cold, jnp.where(chip == owner + done[0, 0], blocks[owner], arrived))

    grad_gate, grad_up, grad_down, hot_grads = lax.switch(
        hot_expert // 2,
        [functools.partial(finish, owner) for owner in range(chips)],
        kept,
        taken,
        near_4,
        side_4,
        second_unit,
        second_swap,
        sources,
    )
    hot_grads = jnp.transpose(hot_grads, (1, 0, 2))
    return (grad_gate[None], grad_up[None], grad_down[None], hot_grads[None])


def solution(mesh):
    placed = (
        P(("dp", "expert"), None),
        P(("dp", "expert"), None),
        P(("dp", "expert")),
        P(("dp", "expert")),
        P(),
        P("expert", None, "dp"),
        P("expert", None, "dp"),
        P("expert", "dp", None),
    )
    return jax.shard_map(
        on_device,
        mesh=mesh,
        in_specs=placed,
        out_specs=(
            P("expert", None, "dp"),
            P("expert", None, "dp"),
            P("expert", "dp", None),
            P(None, "expert", None, "dp"),
        ),
        check_vma=False,
    )
```

```python
import functools

import jax
import jax.numpy as jnp
from jax import lax
from jax.experimental import pallas as pl
from jax.experimental.pallas import tpu as pltpu
from jax.sharding import PartitionSpec as P

CONTRACT_ROWS = (((0,), (0,)), ((), ()))


def spread(block, axis, source):
    block = jnp.where(lax.axis_index(axis) == source, block, jnp.zeros_like(block))
    return lax.psum(block, axis)


def expert_terms(row_tokens, row_grads, gate_matrix, up_matrix, down_matrix):
    pre_gate = jnp.dot(row_tokens, gate_matrix, preferred_element_type=jnp.float32)
    pre_up = jnp.dot(row_tokens, up_matrix, preferred_element_type=jnp.float32)
    hidden_back = lax.dot_general(
        row_grads, down_matrix, (((1,), (1,)), ((), ())), preferred_element_type=jnp.float32
    )
    sigmoid_gate = jax.nn.sigmoid(pre_gate)
    activated = pre_gate * sigmoid_gate
    hidden = (activated * pre_up).astype(jnp.bfloat16)
    gate_grad = (
        hidden_back * pre_up * sigmoid_gate * (1.0 + pre_gate * (1.0 - sigmoid_gate))
    ).astype(jnp.bfloat16)
    up_grad = (hidden_back * activated).astype(jnp.bfloat16)
    return (hidden, gate_grad, up_grad)


def column_sum(left, right):
    return lax.dot_general(left, right, CONTRACT_ROWS, preferred_element_type=jnp.float32)


def route_rows(selector, values):
    return jnp.dot(selector, values, preferred_element_type=jnp.float32).astype(jnp.bfloat16)


def on_large_mesh(tokens, cotangent, gate_scale, expert_index, hot_index, w_gate, w_up, w_down):
    tok_rows, feature_width = tokens.shape
    experts = lax.axis_size("expert")
    capacity = 3 * tok_rows // (2 * experts)
    hot_capacity = 2 * capacity
    hot_expert = hot_index[0]
    route_grad = (gate_scale[:, None] * cotangent.astype(jnp.float32)).astype(jnp.bfloat16)
    is_hot = expert_index == hot_expert
    not_hot = jnp.logical_not(is_hot)
    owners = lax.broadcasted_iota(jnp.int32, (tok_rows, experts), 1)
    member = ((expert_index[:, None] == owners) & not_hot[:, None]).astype(jnp.int32)
    bucket_place = jnp.sum((jnp.cumsum(member, axis=0) - 1) * member, axis=1)
    slot_index = expert_index * capacity + bucket_place
    slot_grid = lax.broadcasted_iota(jnp.int32, (experts * capacity, tok_rows), 0)
    cold_map = ((slot_grid == slot_index[None, :]) & not_hot[None, :]).astype(jnp.bfloat16)
    hot_place = jnp.cumsum(is_hot.astype(jnp.int32)) - 1
    hot_grid = lax.broadcasted_iota(jnp.int32, (hot_capacity, tok_rows), 0)
    hot_map = ((hot_grid == hot_place[None, :]) & is_hot[None, :]).astype(jnp.bfloat16)
    send_tokens = route_rows(cold_map, tokens).reshape(experts, capacity, feature_width)
    send_grads = route_rows(cold_map, route_grad).reshape(experts, capacity, feature_width)
    own_hot_tokens = route_rows(hot_map, tokens)
    own_hot_grads = route_rows(hot_map, route_grad)
    arrived_tokens, arrived_grads = (
        lax.all_to_all(send_tokens, "expert", split_axis=0, concat_axis=0, tiled=True),
        lax.all_to_all(send_grads, "expert", split_axis=0, concat_axis=0, tiled=True),
    )
    cold_tokens, cold_grads, hot_tokens, hot_row_grads = (
        lax.all_gather(
            arrived_tokens.reshape(experts * capacity, feature_width), "dp", axis=0, tiled=True
        ),
        lax.all_gather(
            arrived_grads.reshape(experts * capacity, feature_width), "dp", axis=0, tiled=True
        ),
        lax.all_gather(own_hot_tokens, "dp", axis=0, tiled=True),
        lax.all_gather(own_hot_grads, "dp", axis=0, tiled=True),
    )
    shadow_gate, shadow_up, shadow_down = (
        spread(w_gate[0], "expert", hot_expert),
        spread(w_up[0], "expert", hot_expert),
        spread(w_down[0], "expert", hot_expert),
    )
    hidden, gate_grad, up_grad = expert_terms(
        cold_tokens, cold_grads, w_gate[0], w_up[0], w_down[0]
    )
    grad_gate = column_sum(cold_tokens, gate_grad).astype(jnp.bfloat16)
    grad_up = column_sum(cold_tokens, up_grad).astype(jnp.bfloat16)
    grad_down = column_sum(hidden, cold_grads).astype(jnp.bfloat16)
    hot_hidden, hot_gate_grad, hot_up_grad = expert_terms(
        hot_tokens, hot_row_grads, shadow_gate, shadow_up, shadow_down
    )
    gate_part = column_sum(hot_tokens, hot_gate_grad)
    up_part = column_sum(hot_tokens, hot_up_grad)
    down_part = column_sum(hot_row_grads, hot_hidden)
    owned_part = lax.psum_scatter(
        jnp.stack([gate_part, up_part, down_part], axis=1),
        "expert",
        scatter_dimension=0,
        tiled=True,
    )
    hot_grads = owned_part.astype(jnp.bfloat16)[None]
    return (grad_gate[None], grad_up[None], grad_down[None], hot_grads)


ANYWHERE = pl.BlockSpec(memory_space=pltpu.HBM)
VMEM_LIMIT = 56 * 2**20


def together(passed, awaited=()):
    n = len(passed)
    return pl.pallas_call(
        lambda *refs: None,
        out_shape=[jax.ShapeDtypeStruct(a.shape, a.dtype) for a in passed],
        in_specs=[pl.BlockSpec(memory_space=pl.ANY)] * (n + len(awaited)),
        out_specs=[pl.BlockSpec(memory_space=pl.ANY)] * n,
        input_output_aliases={i: i for i in range(n)},
        name="together",
    )(*passed, *awaited)


def divisor(size, most, unit):
    return max(d for d in range(unit, most + 1, unit) if size % d == 0)


def terms_kernel(kind, plan, n_sources, block_rows, block_columns, *refs):
    flags, refs = refs[0], refs[1:]
    sources, refs = refs[:n_sources], refs[n_sources:]
    sets = 2 if kind == "hot" else 1
    weight_refs, refs = refs[: 3 * sets], refs[3 * sets :]
    in_sem, w_sem, out_sem = refs[-3:]
    refs = refs[:-3]
    if kind == "cold":
        *outs, done, tok, grd, gate_w, up_w, down_w, gate_up_t, hidden_t, res_a, res_b, res_c = refs
    else:
        *outs, tok, grd, gate_w, up_w, down_w, gate_up_t, hidden_t, res_a, res_b, res_c = refs
    rows, width = tok.shape
    hidden_width = gate_w.shape[1]
    core = flags[0]
    column_blocks = width // block_columns

    def copies(choice, core_value, first_piece, last_piece):
        at, result = 0, []
        for k, (by_core, count) in enumerate(plan[choice]):
            if first_piece <= k < last_piece:
                for which, buffer in enumerate((tok, grd)):
                    source, first = by_core[core_value][which]
                    result.append(
                        pltpu.make_async_copy(
                            sources[source].at[pl.ds(first, count)],
                            buffer.at[pl.ds(at, count)],
                            in_sem.at[2 * k + which],
                        )
                    )
            at += count
        return result

    def span_of(i):
        return pl.ds(i * block_columns, block_columns)

    def work():
        def fetched(which):
            return [
                pltpu.make_async_copy(weight_refs[3 * which + i], buffer, w_sem.at[i])
                for i, buffer in enumerate((gate_w, up_w, down_w))
            ]

        weights = fetched(0)
        for which in range(sets):

            @pl.when(flags[3] == which)
            def _():
                for copy in fetched(which):
                    copy.start()

        sizes = [entry[-1] for entry in plan[0]]

        def fetch(first_piece, last_piece):
            for choice in range(len(plan)):
                for core_value in range(2):

                    @pl.when((flags[2] == choice) & (core == core_value))
                    def _():
                        for copy in copies(choice, core_value, first_piece, last_piece):
                            copy.start()

        def needed(block):
            return next(
                k for k in range(len(sizes) + 1) if sum(sizes[:k]) >= (block + 1) * block_rows
            )

        fetch(0, needed(0))
        for copy in weights:
            copy.wait()

        def forward(first_row):
            span = pl.ds(first_row, block_rows)
            row_tokens, row_grads = tok[span, :], grd[span, :]
            pre_gate = jnp.dot(row_tokens, gate_w[...], preferred_element_type=jnp.float32)
            pre_up = jnp.dot(row_tokens, up_w[...], preferred_element_type=jnp.float32)
            hidden_back = lax.dot_general(
                row_grads, down_w[...], (((1,), (1,)), ((), ())), preferred_element_type=jnp.float32
            )
            sigmoid_gate = jax.nn.sigmoid(pre_gate)
            activated = pre_gate * sigmoid_gate
            hidden = activated * pre_up
            gate_grad = hidden_back * pre_up * sigmoid_gate * (1.0 + pre_gate * (1.0 - sigmoid_gate))
            up_grad = hidden_back * activated
            hidden_t[:, span] = hidden.T.astype(jnp.bfloat16)
            gate_up_t[pl.ds(0, hidden_width), span] = gate_grad.T.astype(jnp.bfloat16)
            gate_up_t[pl.ds(hidden_width, hidden_width), span] = up_grad.T.astype(jnp.bfloat16)

        if kind == "cold":
            fetch(needed(0), len(sizes))
            for copy in copies(0, 0, 0, len(sizes)):
                copy.wait()

            def each(i, carry):
                forward(pl.multiple_of(i * block_rows, block_rows))
                return carry

            lax.fori_loop(0, rows // block_rows, each, 0)
        else:
            arrived = 0
            for block in range(rows // block_rows):
                for copy in copies(0, 0, arrived, needed(block)):
                    copy.wait()
                arrived = needed(block)
                if block == 0:
                    fetch(arrived, len(sizes))
                forward(block * block_rows)

        def products(span):
            sums = jnp.dot(gate_up_t[...], tok[:, span], preferred_element_type=jnp.float32)
            downs = jnp.dot(hidden_t[...], grd[:, span], preferred_element_type=jnp.float32)
            return sums, downs

        if kind == "cold":

            def columns(i, carry):
                span = pl.ds(pl.multiple_of(i * block_columns, block_columns), block_columns)
                sums, downs = products(span)
                sums = sums.T.astype(jnp.bfloat16)
                res_a[span, :] = sums[:, :hidden_width]
                res_b[span, :] = sums[:, hidden_width:]
                res_c[:, span] = downs.astype(jnp.bfloat16)
                return carry

            lax.fori_loop(0, column_blocks, columns, 0)
            return
        chips = len(outs)
        part = width // (2 * chips)
        lead = part % 128
        window = part + lead
        for chip in range(chips):
            start = 2 * part * chip + core * (part - lead)
            span = pl.ds(pl.multiple_of(start, 128), window)
            here = pl.ds(chip * window, window)
            sums, downs = products(span)
            sums = sums.T.astype(jnp.bfloat16)
            res_a[here, :] = sums[:, :hidden_width]
            res_b[here, :] = sums[:, hidden_width:]
            res_c[here, :] = downs.T.astype(jnp.bfloat16)
        written = [
            pltpu.make_async_copy(
                res.at[pl.ds(pl.multiple_of(chip * window + core * lead, 16), part)],
                outs[chip].at[q],
                out_sem.at[3 * chip + q],
            )
            for chip in range(chips)
            for q, res in enumerate((res_a, res_b, res_c))
        ]
        for copy in written:
            copy.start()
        for copy in written:
            copy.wait()

    @pl.when(flags[1] == 1)
    def _():
        work()

    if kind == "cold":

        @pl.when(flags[1] == 0)
        def _():
            for res in (res_a, res_b, res_c):
                res[...] = jnp.zeros_like(res)

        written = [
            pltpu.make_async_copy(res, out, out_sem.at[i])
            for i, (res, out) in enumerate(zip((res_a, res_b, res_c), outs))
        ]
        for copy in written:
            copy.start()
        done[...] = jnp.zeros_like(done)
        for copy in written:
            copy.wait()


def expert_call(kind, flags, plan, blocks, sources, weights):
    width, hidden_width = weights[0].shape
    rows = sum(entry[-1] for entry in plan[0])
    block_rows = divisor(rows, 384 if kind == "hot" else 128, 128)
    block_columns = divisor(width, 512 if kind == "hot" else 256, 128)
    bf16 = jnp.bfloat16
    scratch = [
        pltpu.VMEM((rows, width), bf16),
        pltpu.VMEM((rows, width), bf16),
        pltpu.VMEM((width, hidden_width), bf16),
        pltpu.VMEM((width, hidden_width), bf16),
        pltpu.VMEM((hidden_width, width), bf16),
        pltpu.VMEM((2 * hidden_width, rows), bf16),
        pltpu.VMEM((hidden_width, rows), bf16),
    ]
    result = pltpu.VMEM((width, hidden_width), bf16)
    if kind == "hot":
        chips = blocks // 2
        part = width // blocks
        out_shape = [jax.ShapeDtypeStruct((3, part, hidden_width), bf16)] * chips
        result = pltpu.VMEM((chips * (part + part % 128), hidden_width), bf16)
        scratch += [result, result, result]
    else:
        out_shape = [jax.ShapeDtypeStruct(w.shape, bf16) for w in weights[:3]]
        out_shape += [jax.ShapeDtypeStruct((8, 128), jnp.int32)]
        scratch += [result, result, pltpu.VMEM((hidden_width, width), bf16)]
    scratch += [
        pltpu.SemaphoreType.DMA((2 * len(plan[0]),)),
        pltpu.SemaphoreType.DMA((3,)),
        pltpu.SemaphoreType.DMA((3 * blocks,)),
    ]
    out_specs = [ANYWHERE] * len(out_shape)
    if kind == "cold":
        out_specs[-1] = pl.BlockSpec(memory_space=pltpu.VMEM)
    kernel = functools.partial(terms_kernel, kind, plan, len(sources), block_rows, block_columns)
    return pl.pallas_call(
        kernel,
        out_shape=out_shape,
        in_specs=[pl.BlockSpec(memory_space=pltpu.SMEM)]
        + [ANYWHERE] * (len(sources) + len(weights)),
        out_specs=out_specs,
        scratch_shapes=scratch,
        compiler_params=pltpu.CompilerParams(vmem_limit_bytes=VMEM_LIMIT),
        cost_estimate=pl.CostEstimate(
            flops=12 * rows * width * hidden_width,
            bytes_accessed=4 * rows * width + 12 * width * hidden_width,
            transcendentals=rows * hidden_width,
        ),
        name=kind + "_terms",
    )(flags, *sources, *weights)


def on_device(tokens, cotangent, gate_scale, expert_index, hot_index, w_gate, w_up, w_down):
    tok_rows, width = tokens.shape
    experts = lax.axis_size("expert")
    dp = lax.axis_size("dp")
    chips = experts // 2
    capacity = 3 * tok_rows // (2 * experts)
    if chips != 4 or dp != 4 or capacity % 8 != 0:
        return on_large_mesh(
            tokens, cotangent, gate_scale, expert_index, hot_index, w_gate, w_up, w_down
        )
    hot_expert = hot_index[0]
    me = lax.axis_index("expert")
    core, chip = me % 2, me // 2
    flat = [(i, j) for i in range(dp) for j in range(experts)]

    def place_of(i, j):
        return i * experts + j

    def swap(array):
        return lax.ppermute(array, "expert", [(j, j ^ 1) for j in range(experts)])

    def along(array, step):
        return lax.ppermute(array, "expert", [(j, j ^ (2 * step)) for j in range(experts)])

    def first_way(array):
        pairs = [(place_of(i, j), place_of(i ^ (2 if j % 2 else 1), j)) for i, j in flat]
        return lax.ppermute(array, ("dp", "expert"), pairs)

    def second_way(array):
        pairs = [(place_of(i, j), place_of(i ^ (1 if j % 2 else 2), j)) for i, j in flat]
        return lax.ppermute(array, ("dp", "expert"), pairs)

    route_grad = (gate_scale[:, None] * cotangent.astype(jnp.float32)).astype(jnp.bfloat16)
    own = jnp.where(core == 0, tokens, route_grad)
    other = jnp.where(core == 0, route_grad, tokens)
    sibling, sibling_index = swap(other), swap(expert_index)
    earlier = lax.broadcasted_iota(jnp.int32, (tok_rows, tok_rows), 1) < lax.broadcasted_iota(
        jnp.int32, (tok_rows, tok_rows), 0
    )

    def places(index):
        return jnp.sum(((index[:, None] == index[None, :]) & earlier).astype(jnp.int32), axis=1)

    index = jnp.concatenate([expert_index, sibling_index])
    place = jnp.concatenate([places(expert_index), places(sibling_index)])
    holder = jnp.concatenate([jnp.full((tok_rows,), core), jnp.full((tok_rows,), 1 - core)])
    values = jnp.concatenate([own, sibling], axis=0)
    message = 2 * capacity
    slots = lax.broadcasted_iota(jnp.int32, (message, 2 * tok_rows), 0)

    def selector(kind, step):
        target = chip ^ step
        expert = jnp.where(hot_expert // 2 == target, hot_expert, 2 * target)
        offset = 0
        if kind == "second":
            expert = expert ^ 1
        elif kind == "rest":
            expert, offset = hot_expert, capacity
        taken = (index == expert) & (place >= offset) & (place < offset + capacity)
        slot = place - offset + capacity * holder
        return ((slots == slot[None, :]) & taken[None, :]).astype(jnp.bfloat16)

    def rows(*wanted, of=values):
        return route_rows(jnp.concatenate([selector(*w) for w in wanted], axis=0), of)

    weights = (w_gate[0], w_up[0], w_down[0])
    is_owner = me == hot_expert
    owns = is_owner.astype(jnp.int32)
    zero = jnp.zeros((), jnp.int32)
    hot_chip = (hot_expert // 2 == chip).astype(jnp.int32)
    hot_flags = jnp.stack([core, hot_chip, zero, 1 - owns])
    sibling_weights = tuple(swap(w) for w in weights)

    unit_rows, hot_rows = 3 * message, 2 * message
    weights = (w_gate[0], w_up[0], w_down[0])
    is_owner = me == hot_expert
    owns = is_owner.astype(jnp.int32)
    zero = jnp.zeros((), jnp.int32)
    hot_chip = (hot_expert // 2 == chip).astype(jnp.int32)
    hot_flags = jnp.stack([core, hot_chip, zero, 1 - owns])
    sibling_weights = tuple(swap(w) for w in weights)

    lies = (
        (0, ((4, 0), (5, 0), (6, 0), (7, 0))),
        (8, ((12, 0), (13, 0), (14, 0), (22, 0))),
        (15, ((19, 0), (20, 0), (21, 0), (23, 0))),
        (24, ((28, 0), (29, 0), (30, 0), (31, 0))),
    )

    def pieces(unit, first, count):
        chosen = []
        for k, (array, at) in enumerate(lies[unit][1]):
            mine, theirs = (lies[unit][0] + k, first), (array, at + first)
            chosen.append((((mine, theirs), (theirs, mine)), count))
        return tuple(chosen)

    near_unit = rows(("first", 0), ("rest", 0))
    sent = {k: [rows((k, s)) for s in range(1, chips)] for k in ("first", "rest")}


    (near_unit,) = together([near_unit], sibling_weights)
    near_1, side_1 = first_way(near_unit), second_way(near_unit)
    got = [along(block, s) for s, block in enumerate(sent["first"], 1)]
    first_unit = jnp.concatenate(got, axis=0)
    near_unit, near_1, side_1, first_unit, *sent["rest"] = together(
        [near_unit, near_1, side_1, first_unit, *sent["rest"]]
    )
    far_1 = second_way(near_1)
    near_2, side_2 = first_way(first_unit), second_way(first_unit)
    got = [along(block, s) for s, block in enumerate(sent["rest"], 1)]
    (values,) = together([values], got[:1])
    own_second, *sent["second"] = [rows(("second", s), of=values) for s in range(chips)]
    swapped_1 = [swap(a) for a in (near_unit, side_1, near_1)]
    rest_unit = jnp.concatenate(got, axis=0)
    far_1, first_unit, near_2, side_2, rest_unit, *sent["second"] = together([
        far_1, first_unit, near_2, side_2, rest_unit, *sent["second"]
    ])
    far_2 = second_way(near_2)
    near_3, side_3 = first_way(rest_unit), second_way(rest_unit)
    got = [along(block, s) for s, block in enumerate(sent["second"], 1)]
    swapped_1.append(swap(far_1))
    swapped_2 = [swap(a) for a in (first_unit, side_2, near_2)]
    second_unit = jnp.concatenate([own_second] + got, axis=0)
    far_2, rest_unit, near_3, side_3, second_unit, *swapped_1 = together(
        [far_2, rest_unit, near_3, side_3, second_unit, *swapped_1]
    )
    far_3 = second_way(near_3)
    swapped_3 = [swap(a) for a in (rest_unit, side_3, near_3, far_2)]
    far_3, second_unit = together([far_3, second_unit])
    near_4, side_4 = first_way(second_unit), second_way(second_unit)
    far_3_swap = swap(far_3)

    sources = [near_unit, near_1, side_1, far_1, *swapped_1]
    sources += [first_unit, near_2, side_2, far_2, *swapped_2]
    sources += [rest_unit, near_3, side_3, far_3, *swapped_3, far_3_swap]
    kept = expert_call(
        "hot",
        hot_flags,
        (pieces(0, 0, hot_rows) + pieces(1, 0, unit_rows) + pieces(2, 0, unit_rows),),
        experts,
        sources,
        weights + sibling_weights,
    )
    second_swap = swap(second_unit)
    near_4, side_4, second_swap, *kept = together([near_4, side_4, second_swap, *kept])

    first_of_chip = jnp.where(hot_expert // 2 == chip, hot_expert % 2, 0)
    cold_flags = jnp.stack([core, 1 - owns, (first_of_chip != core).astype(jnp.int32), zero])
    first_plan = pieces(0, 0, message)
    for k in range(chips - 1):
        first_plan += pieces(1, k * message, message)
    second_plan = ()
    for k in range(chips):
        second_plan += pieces(3, k * message, message)

    def finish(owner, blocks, near_4, side_4, second_unit, second_swap, sources):
        others = sorted((z for z in range(chips) if z != owner), key=lambda z: -abs(z - owner))

        def send(z):
            pairs = [(2 * owner + c, 2 * z + c) for c in range(2)]
            return lax.ppermute(blocks[z], "expert", pairs)

        far_4 = second_way(near_4)
        near_swap, side_swap = swap(near_4), swap(side_4)
        got = [send(others[0])]
        (far_4,) = together([far_4], got)
        far_swap = swap(far_4)
        got += [send(z) for z in others[1:]]
        *cold, done = expert_call(
            "cold",
            cold_flags,
            (first_plan, second_plan),
            experts,
            sources
            + [second_unit, near_4, side_4, far_4, second_swap, side_swap, near_swap, far_swap],
            weights,
        )
        arrived = functools.reduce(jnp.add, got)
        return (*cold, jnp.where(chip == owner + done[0, 0], blocks[owner], arrived))

    grad_gate, grad_up, grad_down, hot_grads = lax.switch(
        hot_expert // 2,
        [functools.partial(finish, owner) for owner in range(chips)],
        kept,
        near_4,
        side_4,
        second_unit,
        second_swap,
        sources,
    )
    hot_grads = jnp.transpose(hot_grads, (1, 0, 2))
    return (grad_gate[None], grad_up[None], grad_down[None], hot_grads[None])


def solution(mesh):
    placed = (
        P(("dp", "expert"), None),
        P(("dp", "expert"), None),
        P(("dp", "expert")),
        P(("dp", "expert")),
        P(),
        P("expert", None, "dp"),
        P("expert", None, "dp"),
        P("expert", "dp", None),
    )
    return jax.shard_map(
        on_device,
        mesh=mesh,
        in_specs=placed,
        out_specs=(
            P("expert", None, "dp"),
            P("expert", None, "dp"),
            P("expert", "dp", None),
            P(None, "expert", None, "dp"),
        ),
        check_vma=False,
    )
```

```python
import functools

import jax
import jax.numpy as jnp
from jax import lax
from jax.experimental import pallas as pl
from jax.experimental.pallas import tpu as pltpu
from jax.sharding import PartitionSpec as P

CONTRACT_ROWS = (((0,), (0,)), ((), ()))


def spread(block, axis, source):
    block = jnp.where(lax.axis_index(axis) == source, block, jnp.zeros_like(block))
    return lax.psum(block, axis)


def expert_terms(row_tokens, row_grads, gate_matrix, up_matrix, down_matrix):
    pre_gate = jnp.dot(row_tokens, gate_matrix, preferred_element_type=jnp.float32)
    pre_up = jnp.dot(row_tokens, up_matrix, preferred_element_type=jnp.float32)
    hidden_back = lax.dot_general(
        row_grads, down_matrix, (((1,), (1,)), ((), ())), preferred_element_type=jnp.float32
    )
    sigmoid_gate = jax.nn.sigmoid(pre_gate)
    activated = pre_gate * sigmoid_gate
    hidden = (activated * pre_up).astype(jnp.bfloat16)
    gate_grad = (
        hidden_back * pre_up * sigmoid_gate * (1.0 + pre_gate * (1.0 - sigmoid_gate))
    ).astype(jnp.bfloat16)
    up_grad = (hidden_back * activated).astype(jnp.bfloat16)
    return (hidden, gate_grad, up_grad)


def column_sum(left, right):
    return lax.dot_general(left, right, CONTRACT_ROWS, preferred_element_type=jnp.float32)


def route_rows(selector, values):
    return jnp.dot(selector, values, preferred_element_type=jnp.float32).astype(jnp.bfloat16)


def on_large_mesh(tokens, cotangent, gate_scale, expert_index, hot_index, w_gate, w_up, w_down):
    tok_rows, feature_width = tokens.shape
    experts = lax.axis_size("expert")
    capacity = 3 * tok_rows // (2 * experts)
    hot_capacity = 2 * capacity
    hot_expert = hot_index[0]
    route_grad = (gate_scale[:, None] * cotangent.astype(jnp.float32)).astype(jnp.bfloat16)
    is_hot = expert_index == hot_expert
    not_hot = jnp.logical_not(is_hot)
    owners = lax.broadcasted_iota(jnp.int32, (tok_rows, experts), 1)
    member = ((expert_index[:, None] == owners) & not_hot[:, None]).astype(jnp.int32)
    bucket_place = jnp.sum((jnp.cumsum(member, axis=0) - 1) * member, axis=1)
    slot_index = expert_index * capacity + bucket_place
    slot_grid = lax.broadcasted_iota(jnp.int32, (experts * capacity, tok_rows), 0)
    cold_map = ((slot_grid == slot_index[None, :]) & not_hot[None, :]).astype(jnp.bfloat16)
    hot_place = jnp.cumsum(is_hot.astype(jnp.int32)) - 1
    hot_grid = lax.broadcasted_iota(jnp.int32, (hot_capacity, tok_rows), 0)
    hot_map = ((hot_grid == hot_place[None, :]) & is_hot[None, :]).astype(jnp.bfloat16)
    send_tokens = route_rows(cold_map, tokens).reshape(experts, capacity, feature_width)
    send_grads = route_rows(cold_map, route_grad).reshape(experts, capacity, feature_width)
    own_hot_tokens = route_rows(hot_map, tokens)
    own_hot_grads = route_rows(hot_map, route_grad)
    arrived_tokens, arrived_grads = (
        lax.all_to_all(send_tokens, "expert", split_axis=0, concat_axis=0, tiled=True),
        lax.all_to_all(send_grads, "expert", split_axis=0, concat_axis=0, tiled=True),
    )
    cold_tokens, cold_grads, hot_tokens, hot_row_grads = (
        lax.all_gather(
            arrived_tokens.reshape(experts * capacity, feature_width), "dp", axis=0, tiled=True
        ),
        lax.all_gather(
            arrived_grads.reshape(experts * capacity, feature_width), "dp", axis=0, tiled=True
        ),
        lax.all_gather(own_hot_tokens, "dp", axis=0, tiled=True),
        lax.all_gather(own_hot_grads, "dp", axis=0, tiled=True),
    )
    shadow_gate, shadow_up, shadow_down = (
        spread(w_gate[0], "expert", hot_expert),
        spread(w_up[0], "expert", hot_expert),
        spread(w_down[0], "expert", hot_expert),
    )
    hidden, gate_grad, up_grad = expert_terms(
        cold_tokens, cold_grads, w_gate[0], w_up[0], w_down[0]
    )
    grad_gate = column_sum(cold_tokens, gate_grad).astype(jnp.bfloat16)
    grad_up = column_sum(cold_tokens, up_grad).astype(jnp.bfloat16)
    grad_down = column_sum(hidden, cold_grads).astype(jnp.bfloat16)
    hot_hidden, hot_gate_grad, hot_up_grad = expert_terms(
        hot_tokens, hot_row_grads, shadow_gate, shadow_up, shadow_down
    )
    gate_part = column_sum(hot_tokens, hot_gate_grad)
    up_part = column_sum(hot_tokens, hot_up_grad)
    down_part = column_sum(hot_row_grads, hot_hidden)
    owned_part = lax.psum_scatter(
        jnp.stack([gate_part, up_part, down_part], axis=1),
        "expert",
        scatter_dimension=0,
        tiled=True,
    )
    hot_grads = owned_part.astype(jnp.bfloat16)[None]
    return (grad_gate[None], grad_up[None], grad_down[None], hot_grads)


ANYWHERE = pl.BlockSpec(memory_space=pltpu.HBM)
VMEM_LIMIT = 56 * 2**20


def together(passed, awaited=()):
    n = len(passed)
    return pl.pallas_call(
        lambda *refs: None,
        out_shape=[jax.ShapeDtypeStruct(a.shape, a.dtype) for a in passed],
        in_specs=[pl.BlockSpec(memory_space=pl.ANY)] * (n + len(awaited)),
        out_specs=[pl.BlockSpec(memory_space=pl.ANY)] * n,
        input_output_aliases={i: i for i in range(n)},
        name="together",
    )(*passed, *awaited)


def divisor(size, most, unit):
    return max(d for d in range(unit, most + 1, unit) if size % d == 0)


def terms_kernel(kind, plan, n_sources, block_rows, block_columns, *refs):
    flags, refs = refs[0], refs[1:]
    sources, refs = refs[:n_sources], refs[n_sources:]
    sets = 2 if kind == "hot" else 1
    weight_refs, refs = refs[: 3 * sets], refs[3 * sets :]
    in_sem, w_sem, out_sem = refs[-3:]
    refs = refs[:-3]
    if kind == "cold":
        *outs, done, tok, grd, gate_w, up_w, down_w, gate_up_t, hidden_t, res_a, res_b, res_c = refs
    else:
        *outs, tok, grd, gate_w, up_w, down_w, gate_up_t, hidden_t, res_a, res_b, res_c = refs
    rows, width = tok.shape
    hidden_width = gate_w.shape[1]
    core = flags[0]
    column_blocks = width // block_columns

    def copies(choice, core_value, first_piece, last_piece):
        at, result = 0, []
        for k, (by_core, count) in enumerate(plan[choice]):
            if first_piece <= k < last_piece:
                for which, buffer in enumerate((tok, grd)):
                    source, first = by_core[core_value][which]
                    result.append(
                        pltpu.make_async_copy(
                            sources[source].at[pl.ds(first, count)],
                            buffer.at[pl.ds(at, count)],
                            in_sem.at[2 * k + which],
                        )
                    )
            at += count
        return result

    def span_of(i):
        return pl.ds(i * block_columns, block_columns)

    def work():
        def fetched(which):
            return [
                pltpu.make_async_copy(weight_refs[3 * which + i], buffer, w_sem.at[i])
                for i, buffer in enumerate((gate_w, up_w, down_w))
            ]

        weights = fetched(0)
        for which in range(sets):

            @pl.when(flags[3] == which)
            def _():
                for copy in fetched(which):
                    copy.start()

        sizes = [entry[-1] for entry in plan[0]]

        def fetch(first_piece, last_piece):
            for choice in range(len(plan)):
                for core_value in range(2):

                    @pl.when((flags[2] == choice) & (core == core_value))
                    def _():
                        for copy in copies(choice, core_value, first_piece, last_piece):
                            copy.start()

        def needed(block):
            return next(
                k for k in range(len(sizes) + 1) if sum(sizes[:k]) >= (block + 1) * block_rows
            )

        fetch(0, needed(0))
        for copy in weights:
            copy.wait()

        def forward(first_row):
            span = pl.ds(first_row, block_rows)
            row_tokens, row_grads = tok[span, :], grd[span, :]
            pre_gate = jnp.dot(row_tokens, gate_w[...], preferred_element_type=jnp.float32)
            pre_up = jnp.dot(row_tokens, up_w[...], preferred_element_type=jnp.float32)
            hidden_back = lax.dot_general(
                row_grads, down_w[...], (((1,), (1,)), ((), ())), preferred_element_type=jnp.float32
            )
            sigmoid_gate = jax.nn.sigmoid(pre_gate)
            activated = pre_gate * sigmoid_gate
            hidden = activated * pre_up
            gate_grad = hidden_back * pre_up * sigmoid_gate * (1.0 + pre_gate * (1.0 - sigmoid_gate))
            up_grad = hidden_back * activated
            hidden_t[:, span] = hidden.T.astype(jnp.bfloat16)
            gate_up_t[pl.ds(0, hidden_width), span] = gate_grad.T.astype(jnp.bfloat16)
            gate_up_t[pl.ds(hidden_width, hidden_width), span] = up_grad.T.astype(jnp.bfloat16)

        if kind == "cold":
            half = rows // block_rows // 2
            early = needed(half - 1)
            fetch(needed(0), len(sizes))

            def each(i, carry):
                forward(pl.multiple_of(i * block_rows, block_rows))
                return carry

            for copy in copies(0, 0, 0, early):
                copy.wait()
            lax.fori_loop(0, half, each, 0)
            for copy in copies(0, 0, early, len(sizes)):
                copy.wait()
            lax.fori_loop(half, rows // block_rows, each, 0)
        else:
            arrived = 0
            for block in range(rows // block_rows):
                for copy in copies(0, 0, arrived, needed(block)):
                    copy.wait()
                arrived = needed(block)
                if block == 0:
                    fetch(arrived, len(sizes))
                forward(block * block_rows)

        def products(span):
            sums = jnp.dot(gate_up_t[...], tok[:, span], preferred_element_type=jnp.float32)
            downs = jnp.dot(hidden_t[...], grd[:, span], preferred_element_type=jnp.float32)
            return sums, downs

        if kind == "cold":

            def columns(i, carry):
                span = pl.ds(pl.multiple_of(i * block_columns, block_columns), block_columns)
                sums, downs = products(span)
                sums = sums.T.astype(jnp.bfloat16)
                res_a[span, :] = sums[:, :hidden_width]
                res_b[span, :] = sums[:, hidden_width:]
                res_c[:, span] = downs.astype(jnp.bfloat16)
                return carry

            lax.fori_loop(0, column_blocks, columns, 0)
            return
        chips = len(outs)
        part = width // (2 * chips)
        lead = part % 128
        window = part + lead
        for chip in range(chips):
            start = 2 * part * chip + core * (part - lead)
            span = pl.ds(pl.multiple_of(start, 128), window)
            here = pl.ds(chip * window, window)
            sums, downs = products(span)
            sums = sums.T.astype(jnp.bfloat16)
            res_a[here, :] = sums[:, :hidden_width]
            res_b[here, :] = sums[:, hidden_width:]
            res_c[here, :] = downs.T.astype(jnp.bfloat16)
        written = [
            pltpu.make_async_copy(
                res.at[pl.ds(pl.multiple_of(chip * window + core * lead, 16), part)],
                outs[chip].at[q],
                out_sem.at[3 * chip + q],
            )
            for chip in range(chips)
            for q, res in enumerate((res_a, res_b, res_c))
        ]
        for copy in written:
            copy.start()
        for copy in written:
            copy.wait()

    @pl.when(flags[1] == 1)
    def _():
        work()

    if kind == "cold":

        @pl.when(flags[1] == 0)
        def _():
            for res in (res_a, res_b, res_c):
                res[...] = jnp.zeros_like(res)

        written = [
            pltpu.make_async_copy(res, out, out_sem.at[i])
            for i, (res, out) in enumerate(zip((res_a, res_b, res_c), outs))
        ]
        for copy in written:
            copy.start()
        done[...] = jnp.zeros_like(done)
        for copy in written:
            copy.wait()


def expert_call(kind, flags, plan, blocks, sources, weights):
    width, hidden_width = weights[0].shape
    rows = sum(entry[-1] for entry in plan[0])
    block_rows = divisor(rows, 384 if kind == "hot" else 128, 128)
    block_columns = divisor(width, 512, 128)
    bf16 = jnp.bfloat16
    scratch = [
        pltpu.VMEM((rows, width), bf16),
        pltpu.VMEM((rows, width), bf16),
        pltpu.VMEM((width, hidden_width), bf16),
        pltpu.VMEM((width, hidden_width), bf16),
        pltpu.VMEM((hidden_width, width), bf16),
        pltpu.VMEM((2 * hidden_width, rows), bf16),
        pltpu.VMEM((hidden_width, rows), bf16),
    ]
    result = pltpu.VMEM((width, hidden_width), bf16)
    if kind == "hot":
        chips = blocks // 2
        part = width // blocks
        out_shape = [jax.ShapeDtypeStruct((3, part, hidden_width), bf16)] * chips
        result = pltpu.VMEM((chips * (part + part % 128), hidden_width), bf16)
        scratch += [result, result, result]
    else:
        out_shape = [jax.ShapeDtypeStruct(w.shape, bf16) for w in weights[:3]]
        out_shape += [jax.ShapeDtypeStruct((8, 128), jnp.int32)]
        scratch += [result, result, pltpu.VMEM((hidden_width, width), bf16)]
    scratch += [
        pltpu.SemaphoreType.DMA((2 * len(plan[0]),)),
        pltpu.SemaphoreType.DMA((3,)),
        pltpu.SemaphoreType.DMA((3 * blocks,)),
    ]
    out_specs = [ANYWHERE] * len(out_shape)
    if kind == "cold":
        out_specs[-1] = pl.BlockSpec(memory_space=pltpu.VMEM)
    kernel = functools.partial(terms_kernel, kind, plan, len(sources), block_rows, block_columns)
    return pl.pallas_call(
        kernel,
        out_shape=out_shape,
        in_specs=[pl.BlockSpec(memory_space=pltpu.SMEM)]
        + [ANYWHERE] * (len(sources) + len(weights)),
        out_specs=out_specs,
        scratch_shapes=scratch,
        compiler_params=pltpu.CompilerParams(vmem_limit_bytes=VMEM_LIMIT),
        cost_estimate=pl.CostEstimate(
            flops=12 * rows * width * hidden_width,
            bytes_accessed=4 * rows * width + 12 * width * hidden_width,
            transcendentals=rows * hidden_width,
        ),
        name=kind + "_terms",
    )(flags, *sources, *weights)


def on_device(tokens, cotangent, gate_scale, expert_index, hot_index, w_gate, w_up, w_down):
    tok_rows, width = tokens.shape
    experts = lax.axis_size("expert")
    dp = lax.axis_size("dp")
    chips = experts // 2
    capacity = 3 * tok_rows // (2 * experts)
    if chips != 4 or dp != 4 or capacity % 8 != 0:
        return on_large_mesh(
            tokens, cotangent, gate_scale, expert_index, hot_index, w_gate, w_up, w_down
        )
    hot_expert = hot_index[0]
    me = lax.axis_index("expert")
    core, chip = me % 2, me // 2
    flat = [(i, j) for i in range(dp) for j in range(experts)]

    def place_of(i, j):
        return i * experts + j

    def swap(array):
        return lax.ppermute(array, "expert", [(j, j ^ 1) for j in range(experts)])

    def along(array, step):
        return lax.ppermute(array, "expert", [(j, j ^ (2 * step)) for j in range(experts)])

    def first_way(array):
        pairs = [(place_of(i, j), place_of(i ^ (2 if j % 2 else 1), j)) for i, j in flat]
        return lax.ppermute(array, ("dp", "expert"), pairs)

    def second_way(array):
        pairs = [(place_of(i, j), place_of(i ^ (1 if j % 2 else 2), j)) for i, j in flat]
        return lax.ppermute(array, ("dp", "expert"), pairs)

    route_grad = (gate_scale[:, None] * cotangent.astype(jnp.float32)).astype(jnp.bfloat16)
    own = jnp.where(core == 0, tokens, route_grad)
    other = jnp.where(core == 0, route_grad, tokens)
    sibling, sibling_index = swap(other), swap(expert_index)
    earlier = lax.broadcasted_iota(jnp.int32, (tok_rows, tok_rows), 1) < lax.broadcasted_iota(
        jnp.int32, (tok_rows, tok_rows), 0
    )

    def places(index):
        return jnp.sum(((index[:, None] == index[None, :]) & earlier).astype(jnp.int32), axis=1)

    index = jnp.concatenate([expert_index, sibling_index])
    place = jnp.concatenate([places(expert_index), places(sibling_index)])
    holder = jnp.concatenate([jnp.full((tok_rows,), core), jnp.full((tok_rows,), 1 - core)])
    values = jnp.concatenate([own, sibling], axis=0)
    message = 2 * capacity
    slots = lax.broadcasted_iota(jnp.int32, (message, 2 * tok_rows), 0)

    def selector(kind, step):
        target = chip ^ step
        expert = jnp.where(hot_expert // 2 == target, hot_expert, 2 * target)
        offset = 0
        if kind == "second":
            expert = expert ^ 1
        elif kind == "rest":
            expert, offset = hot_expert, capacity
        taken = (index == expert) & (place >= offset) & (place < offset + capacity)
        slot = place - offset + capacity * holder
        return ((slots == slot[None, :]) & taken[None, :]).astype(jnp.bfloat16)

    def rows(*wanted):
        return route_rows(jnp.concatenate([selector(*w) for w in wanted], axis=0), values)

    weights = (w_gate[0], w_up[0], w_down[0])
    is_owner = me == hot_expert
    owns = is_owner.astype(jnp.int32)
    zero = jnp.zeros((), jnp.int32)
    hot_chip = (hot_expert // 2 == chip).astype(jnp.int32)
    hot_flags = jnp.stack([core, hot_chip, zero, 1 - owns])
    sibling_weights = tuple(swap(w) for w in weights)

    unit_rows, hot_rows = 3 * message, 2 * message
    weights = (w_gate[0], w_up[0], w_down[0])
    is_owner = me == hot_expert
    owns = is_owner.astype(jnp.int32)
    zero = jnp.zeros((), jnp.int32)
    hot_chip = (hot_expert // 2 == chip).astype(jnp.int32)
    hot_flags = jnp.stack([core, hot_chip, zero, 1 - owns])
    sibling_weights = tuple(swap(w) for w in weights)

    lies = (
        (0, ((4, 0), (5, 0), (6, 0), (7, 0))),
        (8, ((12, 0), (13, 0), (14, 0), (22, 0))),
        (15, ((19, 0), (20, 0), (21, 0), (23, 0))),
        (24, ((28, 0), (29, 0), (30, 0), (31, 0))),
    )

    def pieces(unit, first, count):
        chosen = []
        for k, (array, at) in enumerate(lies[unit][1]):
            mine, theirs = (lies[unit][0] + k, first), (array, at + first)
            chosen.append((((mine, theirs), (theirs, mine)), count))
        return tuple(chosen)

    near_unit = rows(("first", 0), ("rest", 0))
    sent = {k: [rows((k, s)) for s in range(1, chips)] for k in ("first", "rest", "second")}
    own_second = rows(("second", 0))


    (near_unit,) = together([near_unit], sibling_weights)
    near_1, side_1 = first_way(near_unit), second_way(near_unit)
    got = [along(block, s) for s, block in enumerate(sent["first"], 1)]
    first_unit = jnp.concatenate(got, axis=0)
    near_unit, near_1, side_1, first_unit, *held = together(
        [near_unit, near_1, side_1, first_unit, *sent["rest"], *sent["second"]]
    )
    sent["rest"], sent["second"] = held[: chips - 1], held[chips - 1 :]
    far_1 = second_way(near_1)
    near_2, side_2 = first_way(first_unit), second_way(first_unit)
    got = [along(block, s) for s, block in enumerate(sent["rest"], 1)]
    swapped_1 = [swap(a) for a in (near_unit, side_1, near_1)]
    rest_unit = jnp.concatenate(got, axis=0)
    far_1, first_unit, near_2, side_2, rest_unit, *sent["second"] = together([
        far_1, first_unit, near_2, side_2, rest_unit, *sent["second"]
    ])
    far_2 = second_way(near_2)
    near_3, side_3 = first_way(rest_unit), second_way(rest_unit)
    got = [along(block, s) for s, block in enumerate(sent["second"], 1)]
    swapped_1.append(swap(far_1))
    swapped_2 = [swap(a) for a in (first_unit, side_2, near_2)]
    second_unit = jnp.concatenate([own_second] + got, axis=0)
    far_2, rest_unit, near_3, side_3, second_unit, *swapped_1 = together(
        [far_2, rest_unit, near_3, side_3, second_unit, *swapped_1]
    )
    far_3 = second_way(near_3)
    swapped_3 = [swap(a) for a in (rest_unit, side_3, near_3, far_2)]
    far_3, second_unit = together([far_3, second_unit])
    near_4, side_4 = first_way(second_unit), second_way(second_unit)
    far_3_swap = swap(far_3)

    sources = [near_unit, near_1, side_1, far_1, *swapped_1]
    sources += [first_unit, near_2, side_2, far_2, *swapped_2]
    sources += [rest_unit, near_3, side_3, far_3, *swapped_3, far_3_swap]
    kept = expert_call(
        "hot",
        hot_flags,
        (pieces(0, 0, hot_rows) + pieces(1, 0, unit_rows) + pieces(2, 0, unit_rows),),
        experts,
        sources,
        weights + sibling_weights,
    )
    second_swap = swap(second_unit)
    near_4, side_4, second_swap, *kept = together([near_4, side_4, second_swap, *kept])

    first_of_chip = jnp.where(hot_expert // 2 == chip, hot_expert % 2, 0)
    cold_flags = jnp.stack([core, 1 - owns, (first_of_chip != core).astype(jnp.int32), zero])
    first_plan = pieces(0, 0, message)
    for k in range(chips - 1):
        first_plan += pieces(1, k * message, message)
    second_plan = ()
    for k in range(chips):
        second_plan += pieces(3, k * message, message)

    def finish(owner, blocks, near_4, side_4, second_unit, second_swap, sources):
        others = sorted((z for z in range(chips) if z != owner), key=lambda z: -abs(z - owner))

        def send(z):
            pairs = [(2 * owner + c, 2 * z + c) for c in range(2)]
            return lax.ppermute(blocks[z], "expert", pairs)

        far_4 = second_way(near_4)
        near_swap, side_swap = swap(near_4), swap(side_4)
        got = [send(others[0])]
        (far_4,) = together([far_4], got)
        far_swap = swap(far_4)
        got += [send(z) for z in others[1:]]
        *cold, done = expert_call(
            "cold",
            cold_flags,
            (first_plan, second_plan),
            experts,
            sources
            + [second_unit, near_4, side_4, far_4, second_swap, side_swap, near_swap, far_swap],
            weights,
        )
        arrived = functools.reduce(jnp.add, got)
        return (*cold, jnp.where(chip == owner + done[0, 0], blocks[owner], arrived))

    grad_gate, grad_up, grad_down, hot_grads = lax.switch(
        hot_expert // 2,
        [functools.partial(finish, owner) for owner in range(chips)],
        kept,
        near_4,
        side_4,
        second_unit,
        second_swap,
        sources,
    )
    hot_grads = jnp.transpose(hot_grads, (1, 0, 2))
    return (grad_gate[None], grad_up[None], grad_down[None], hot_grads[None])


def solution(mesh):
    placed = (
        P(("dp", "expert"), None),
        P(("dp", "expert"), None),
        P(("dp", "expert")),
        P(("dp", "expert")),
        P(),
        P("expert", None, "dp"),
        P("expert", None, "dp"),
        P("expert", "dp", None),
    )
    return jax.shard_map(
        on_device,
        mesh=mesh,
        in_specs=placed,
        out_specs=(
            P("expert", None, "dp"),
            P("expert", None, "dp"),
            P("expert", "dp", None),
            P(None, "expert", None, "dp"),
        ),
        check_vma=False,
    )
```
